256 devices in a mesh: grp: 2 (over core), seq: 32 (over x, z_lo, y), head: 4 (over z_hi).
Axes of the slice: x: 4, y: 4, z: 8 (z_hi: 4, z_lo: 2; z = z_hi * 2 + z_lo), core: 2. Of those that a mesh axis runs over, the one named last changes fastest.
Arguments:
- queries: bfloat16 [1024, 2048], P(('grp', 'seq'), 'head'), may hold values from -100 to 100
- keys: bfloat16 [2, 32768, 2048], P(None, ('grp', 'seq'), 'head'), may hold values from -15 to 15
- values: bfloat16 [2, 32768, 2048], P(None, ('grp', 'seq'), 'head'), may hold values from -6 to 6
- grad_out: bfloat16 [1024, 2048], P(('grp', 'seq', 'head')), may hold values from -6 to 6
- pad_counts: int32 [2], replicated, may hold values from 0 to 256, as said below
Outputs:
- context: bfloat16 [1024, 2048], P(('grp', 'seq', 'head'))
- grad_queries: bfloat16 [1024, 2048], P(('grp', 'seq'), 'head')
- grad_keys: bfloat16 [2, 32768, 2048], P(None, ('grp', 'seq'), 'head')
- grad_values: bfloat16 [2, 32768, 2048], P(None, ('grp', 'seq'), 'head')
The draws below stay inside these ranges and needn't reach their ends.
Inputs may be any that keep to these rules, and one draw needn't show every extreme that they name: `pad_counts`: each count is at most 256, and in every draw one pair has exactly 256 padding tokens.
All inputs are finite; a program needn't handle non-finite values.
Results may differ from the reference program's by a relative error of at most 0.0215.
Values may be sent and summed in bfloat16 or wider, within the bound.
A program may use at most 64 MiB of HBM per device.

```python
import math
import jax
import jax.numpy as jnp
from jax import lax

HEADS = 32
HEAD_DIM = 64
BATCH = 2
TGT = 512
SRC = 32768


def key_table(key):
    rows = jax.random.normal(jax.random.fold_in(key, 5), (BATCH, SRC, HEADS * HEAD_DIM), jnp.float32) * 2.5
    rows = jnp.clip(rows, -15.0, 15.0)
    return rows


def draw_keys(key, part):
    return key_table(key).astype(jnp.bfloat16)


def draw_queries(key, part):
    key = jax.random.fold_in(key, 7)
    total_rows = BATCH * TGT
    width = HEADS * HEAD_DIM
    base = jnp.clip(jax.random.normal(key, (total_rows, width), jnp.float32), -6.0, 6.0)
    spread = 12.0
    loud = jax.random.randint(jax.random.fold_in(key, 1), (total_rows, 1), 0, 4, jnp.int32) == 0
    strong = jnp.clip(jax.random.normal(jax.random.fold_in(key, 2), (total_rows, width), jnp.float32) * spread, -100.0, 100.0)
    base = jnp.where(loud, strong, base)
    return base.astype(jnp.bfloat16)


def draw_pad_counts(key, part):
    key = jax.random.fold_in(key, 9)
    most = TGT // 2
    counts = jax.random.randint(key, (BATCH,), 0, most + 1, jnp.int32)
    first = jax.random.randint(jax.random.fold_in(key, 1), (), 0, BATCH, jnp.int32)
    index = jnp.arange(BATCH, dtype=jnp.int32)
    return jnp.where(index == first, most, counts)


def shard_levels(stream_key, dims, split, low, high):
    level = 1.0
    for dim, parts in split:
        draws = jax.random.uniform(jax.random.fold_in(jax.random.fold_in(stream_key, 6), dim), (parts,), jnp.float32, low / len(split), high / len(split))
        level = level * jnp.repeat(jnp.exp(draws), dims[dim] // parts).reshape((-1,) + (1,) * (len(dims) - 1 - dim))
    return level


def scatter_about(stream_key, extent, scale, reach, pieces=(), held_as=jnp.bfloat16):
    gain = shard_levels(stream_key, extent, pieces, -0.22, 0.18) if pieces else 1.0
    values = jax.random.normal(stream_key, extent, jnp.float32) * scale * gain
    return jnp.minimum(jnp.maximum(values, -reach), reach).astype(held_as)


def setup_inputs(seed: int = 0) -> dict:
    arg_keys = jax.random.split(jax.random.key(seed), 6)
    queries = draw_queries(jax.random.fold_in(arg_keys[5], 71), 0)
    keys = draw_keys(jax.random.fold_in(arg_keys[5], 71), 0)
    values = scatter_about(arg_keys[2], (BATCH, SRC, HEADS * HEAD_DIM), 1.0, 6.0, ((1, 64), (2, 4)))
    grad_out = scatter_about(arg_keys[3], (BATCH * TGT, HEADS * HEAD_DIM), 1.0, 6.0, ((0, 256),))
    pad_counts = draw_pad_counts(jax.random.fold_in(arg_keys[5], 71), 0)
    return dict(queries=queries, keys=keys, values=values, grad_out=grad_out, pad_counts=pad_counts)


def reference(queries, keys, values, grad_out, pad_counts):
    scale = 1.0 / math.sqrt(HEAD_DIM)
    width = HEADS * HEAD_DIM
    position = jnp.arange(TGT, dtype=jnp.int32)
    block = math.gcd(TGT, 64)
    count = TGT // block
    contexts = []
    query_grads = []
    key_grads = []
    value_grads = []
    for pair in range(BATCH):
        valid = (position < TGT - pad_counts[pair]).astype(jnp.float32)
        key_rows = keys[pair].astype(jnp.float32).reshape(SRC, HEADS, HEAD_DIM)
        value_rows = values[pair].astype(jnp.float32).reshape(SRC, HEADS, HEAD_DIM)
        query_blocks = queries[pair * TGT:(pair + 1) * TGT].reshape(count, block, HEADS, HEAD_DIM)
        grad_blocks = grad_out[pair * TGT:(pair + 1) * TGT].reshape(count, block, HEADS, HEAD_DIM)
        valid_blocks = valid.reshape(count, block)

        def step(carry, item):
            grad_k, grad_v = carry
            query, grad, mask = item
            query = query.astype(jnp.float32)
            scores = jnp.einsum('thd,phd->htp', query, key_rows) * scale
            top = lax.optimization_barrier(jnp.max(scores, axis=-1, keepdims=True))
            expo = jnp.exp(scores - top)
            probs = expo / lax.optimization_barrier(jnp.sum(expo, axis=-1, keepdims=True))
            weights = lax.optimization_barrier(probs.astype(jnp.bfloat16)).astype(jnp.float32)
            attended = jnp.einsum('htp,phd->thd', weights, value_rows) * mask[:, None, None]
            masked = grad.astype(jnp.float32) * mask[:, None, None]
            delta = lax.optimization_barrier(jnp.sum(masked * attended, axis=-1)).T
            grad_probs = jnp.einsum('thd,phd->htp', masked, value_rows)
            grad_scores = (probs * (grad_probs - delta[:, :, None]) * scale).astype(jnp.bfloat16)
            grad_scores = lax.optimization_barrier(grad_scores).astype(jnp.float32)
            grad_q = jnp.einsum('htp,phd->thd', grad_scores, key_rows)
            grad_k = grad_k + jnp.einsum('htp,thd->phd', grad_scores, query)
            grad_v = grad_v + jnp.einsum('htp,thd->phd', weights, masked)
            return ((grad_k, grad_v), (attended.astype(jnp.bfloat16), grad_q.astype(jnp.bfloat16)))
        start = (jnp.zeros((SRC, HEADS, HEAD_DIM), jnp.float32), jnp.zeros((SRC, HEADS, HEAD_DIM), jnp.float32))
        (grad_k, grad_v), (context, grad_q) = lax.scan(step, start, (query_blocks, grad_blocks, valid_blocks))
        contexts.append(context.reshape(TGT, width))
        query_grads.append(grad_q.reshape(TGT, width))
        key_grads.append(grad_k.reshape(SRC, width).astype(jnp.bfloat16))
        value_grads.append(grad_v.reshape(SRC, width).astype(jnp.bfloat16))
    return (jnp.concatenate(contexts, axis=0), jnp.concatenate(query_grads, axis=0), jnp.stack(key_grads, axis=0), jnp.stack(value_grads, axis=0))
```

```python
import jax
import jax.numpy as jnp
from jax import lax
from jax.experimental import pallas as pl
from jax.experimental.pallas import tpu as pltpu
from jax.sharding import PartitionSpec as P

MESH = pl.DeviceIdType.MESH
CHIPS = 32
PEERS = CHIPS - 1
BF = jnp.bfloat16
F32 = jnp.float32


def peer_of(me, i):
    x, z, y = me // 8, (me // 4) % 2, me % 4
    return ((x + i // 8) % 4) * 8 + ((z + (i // 4) % 2) % 2) * 4 + (y + i % 4) % 4


def stat_owner(u):
    x, k = u % 4, u // 4
    return x * 8 + (k % 2) * 4 + (k + x) % 4


def dot(a, b):
    return lax.dot_general(a, b, (((1,), (0,)), ((), ())), preferred_element_type=F32)


def dot_nt(a, b):
    return lax.dot_general(a, b, (((1,), (1,)), ((), ())), preferred_element_type=F32)


def columns(hp):
    return pl.ds(pl.multiple_of(hp * 128, 128), 128)


def kernel(
    pad_ref, q_ref, k_ref, v_ref, g_ref,
    ctx_ref, dq_ref, dk_ref, dv_ref,
    gsend, grecv, gmine, qall, gall, qt_s, gt_s, vkt, ep, oab,
    st, stsib, cst, strecv, resall, obuf, sibbuf, rsbuf, crecv,
    hsem, gat_s, gat_r, sib_s, sib_r, ss_s, ss_r, sr_s, sr_r, rs_s, rs_r, csem,
):
    core = lax.axis_index("grp")
    me = lax.axis_index("seq")
    head = lax.axis_index("head")
    other = 1 - core
    sibling = {"grp": other}

    barrier = pltpu.get_barrier_semaphore()

    @pl.loop(1, CHIPS)
    def _(i):
        pl.semaphore_signal(barrier, inc=1, device_id={"seq": peer_of(me, i)}, device_id_type=MESH)

    pl.semaphore_signal(barrier, inc=1, device_id=sibling, device_id_type=MESH)
    for j in (1, 2, 3):
        pl.semaphore_signal(barrier, inc=1, device_id={"head": (head + j) % 4}, device_id_type=MESH)

    @pl.loop(0, 8)
    def _(i):
        pair, hp = i // 4, i % 4
        kt = k_ref[pair, :, columns(hp)].T
        vt = v_ref[pair, :, columns(hp)].T
        for hh in range(2):
            vkt[pair, 2 * hp + hh, 0:64, :] = vt[64 * hh : 64 * hh + 64]
            vkt[pair, 2 * hp + hh, 64:128, :] = kt[64 * hh : 64 * hh + 64]
            vkt[pair, 2 * hp + hh, 128:144, :] = jnp.ones((16, 512), BF)

    place = (
        lax.broadcasted_iota(jnp.int32, (16, 4), 0) == lax.broadcasted_iota(jnp.int32, (16, 4), 1) + 4 * head
    ).astype(BF)
    for p in range(4):
        gsend[p] = dot(place, g_ref[:, p * 512 : (p + 1) * 512]).astype(BF)

    pl.semaphore_wait(barrier, PEERS + 4)

    def to_head(src, dst, sems, j):
        p = (head + j) % 4
        return pltpu.make_async_remote_copy(
            src(p), dst.at[head], sems.at[j], sems.at[4 + head], device_id={"head": p}, device_id_type=MESH
        )

    def from_head(src, dst, sems, j):
        p = (head + j) % 4
        return pltpu.make_async_remote_copy(
            src(p), dst.at[p], sems.at[j], sems.at[4 + p], device_id={"head": p}, device_id_type=MESH
        )

    def spread(src, dst, send, recv):
        @pl.loop(1, CHIPS)
        def _(i):
            p = peer_of(me, i)
            pltpu.make_async_remote_copy(
                src(p), dst.at[me], send, recv, device_id={"seq": p}, device_id_type=MESH
            ).start()

    def landed(dst, send, recv):
        whole = dst.at[pl.ds(0, PEERS)]
        copy = pltpu.make_async_remote_copy(
            whole, whole, send, recv, device_id=sibling, device_id_type=MESH
        )
        copy.wait_recv()
        copy.wait_send()

    def across(src, dst, k):
        return pltpu.make_async_remote_copy(
            src, dst, sib_s.at[k], sib_r.at[k], device_id=sibling, device_id_type=MESH
        )

    for j in (1, 2, 3):
        to_head(lambda p: gsend.at[p], grecv, hsem, j).start()
    spread(lambda p: q_ref, qall.at[0], gat_s.at[0], gat_r.at[0])
    qall[0, me] = q_ref[...]
    grecv[head] = gsend[head]
    for j in (1, 2, 3):
        from_head(lambda p: gsend.at[p], grecv, hsem, j).wait()

    pad_mine = pad_ref[core]
    token = lax.broadcasted_iota(jnp.int32, (16, 512), 0) + me * 16
    valid = token < 512 - pad_mine
    gsum = (grecv[0].astype(F32) + grecv[1].astype(F32)) + (grecv[2].astype(F32) + grecv[3].astype(F32))
    gown = jnp.where(valid, gsum, 0.0).astype(BF)
    gmine[...] = gown
    spread(lambda p: gmine, gall.at[0], gat_s.at[1], gat_r.at[1])
    gall[0, me] = gown

    longer = jnp.where(pad_ref[1] < pad_ref[0], 1, 0)
    mine_longer = longer == core
    third_slot = jnp.where(mine_longer, 0, 1)

    row = lax.broadcasted_iota(jnp.int32, (128, 256), 0)

    def only(t, hh):
        return jnp.where((row < 64) if hh == 0 else (row >= 64), t, jnp.zeros((), t.dtype))

    def forward(blk, pair, slot, half):
        @pl.loop(0, 4)
        def _(hp):
            q = qall[slot, half * 16 : half * 16 + 16, :, columns(hp)].reshape(256, 128)
            qt = (q * jnp.asarray(0.125, BF)).T
            qt_s[blk, hp] = qt
            k = k_ref[pair, :, columns(hp)]
            for hh in range(2):
                s = dot(k, only(qt, hh))
                m = jnp.max(s, axis=0, keepdims=True)
                p = jnp.exp(s - m).astype(BF)
                ep[blk, 2 * hp + hh, :, 256:512] = p
                ob = dot(vkt[pair, 2 * hp + hh], p)
                oab[blk, hp, hh, 0:128, :] = ob[0:128]
                st[blk, hp, 3 * hh : 3 * hh + 1, :] = m
                st[blk, hp, 3 * hh + 1 : 3 * hh + 2, :] = ob[128:129]

    def backward(blk, pair, slot, half):
        @pl.loop(0, 4)
        def _(hp):
            gt = gall[slot, half * 16 : half * 16 + 16, :, columns(hp)].reshape(256, 128).T
            gt_s[blk, hp] = gt
            v = v_ref[pair, :, columns(hp)]
            for hh in range(2):
                dp = dot(v, only(gt, hh))
                o = oab[blk, hp, hh, 0:64, :]
                r = jnp.sum(gt[64 * hh : 64 * hh + 64].astype(F32) * o, axis=0, keepdims=True)
                l = st[blk, hp, 3 * hh + 1 : 3 * hh + 2, :]
                e = (ep[blk, 2 * hp + hh, :, 256:512].astype(F32) * (dp - r / l)).astype(BF)
                ep[blk, 2 * hp + hh, :, 0:256] = e
                oab[blk, hp, hh, 128:192, :] = dot(vkt[pair, 2 * hp + hh, 64:128, :], e)
                st[blk, hp, 3 * hh + 2 : 3 * hh + 3, :] = r

    landed(qall.at[0], gat_s.at[0], gat_r.at[0])
    send_q = across(qall.at[0], qall.at[1], 0)
    send_q.start()
    forward(0, core, 0, 0)
    landed(gall.at[0], gat_s.at[1], gat_r.at[1])
    send_g = across(gall.at[0], gall.at[1], 1)
    send_g.start()
    send_q.wait()
    forward(1, other, 1, 0)
    forward(2, longer, third_slot, 1)
    send_g.wait()
    backward(1, other, 1, 0)
    backward(2, longer, third_slot, 1)
    backward(0, core, 0, 0)

    stat_a = across(st.at[1], stsib.at[pl.ds(0, 4)], 2)
    stat_b = across(st.at[2, pl.ds(2 * other, 2)], stsib.at[pl.ds(4, 2)], 3)
    stat_a.start()
    stat_b.start()
    stat_a.wait()
    stat_b.wait()

    @pl.loop(0, 6)
    def _(i):
        first = jnp.where(i < 4, 0, 2)
        hp = jnp.where(i < 4, i, 2 * core + i - 4)
        a = st[first, hp]
        b = stsib[i]
        for hh in range(2):
            ma, mb = a[3 * hh : 3 * hh + 1], b[3 * hh : 3 * hh + 1]
            m = jnp.maximum(ma, mb)
            wa, wb = jnp.exp(ma - m), jnp.exp(mb - m)
            rows = (
                m,
                wa * a[3 * hh + 1 : 3 * hh + 2] + wb * b[3 * hh + 1 : 3 * hh + 2],
                wa * a[3 * hh + 2 : 3 * hh + 3] + wb * b[3 * hh + 2 : 3 * hh + 3],
            )
            for j in range(3):
                cst[2 * i, 3 * hh + j : 3 * hh + j + 1, :] = rows[j][:, 0:128]
                cst[2 * i + 1, 3 * hh + j : 3 * hh + j + 1, :] = rows[j][:, 128:256]

    @pl.loop(0, 12)
    def _(u):
        to = stat_owner(u)

        @pl.when(to != me)
        def _():
            pltpu.make_async_remote_copy(
                cst.at[u], strecv.at[me], ss_s.at[u], ss_r, device_id={"seq": to}, device_id_type=MESH
            ).start()

        @pl.when(to == me)
        def _():
            strecv[me] = cst[u]

    xx, zz, yy = me // 8, (me // 4) % 2, me % 4
    kk = (yy - xx + 4) % 4
    is_owner = jnp.logical_and(kk < 3, zz == kk % 2)
    unit = kk * 4 + xx

    @pl.when(is_owner)
    def _():
        whole = strecv.at[pl.ds(0, PEERS)]
        pltpu.make_async_remote_copy(
            whole, whole, ss_s.at[0], ss_r, device_id=sibling, device_id_type=MESH
        ).wait_recv()
        for hh in range(2):
            m = strecv[:, 3 * hh, :]
            top = jnp.max(m, axis=0, keepdims=True)
            w = jnp.exp(m - top)
            inv = 1.0 / jnp.sum(w * strecv[:, 3 * hh + 1, :], axis=0, keepdims=True)
            delta = jnp.sum(w * strecv[:, 3 * hh + 2, :], axis=0, keepdims=True) * inv
            resall[0, unit, 3 * hh : 3 * hh + 1, :] = top
            resall[0, unit, 3 * hh + 1 : 3 * hh + 2, :] = inv
            resall[0, unit, 3 * hh + 2 : 3 * hh + 3, :] = delta

        @pl.loop(1, CHIPS)
        def _(i):
            pltpu.make_async_remote_copy(
                resall.at[0, unit], resall.at[0, unit], sr_s, sr_r.at[unit],
                device_id={"seq": peer_of(me, i)}, device_id_type=MESH,
            ).start()

    @pl.loop(0, 12)
    def _(u):
        to = stat_owner(u)

        @pl.when(to != me)
        def _():
            pltpu.make_async_remote_copy(
                cst.at[u], strecv.at[me], ss_s.at[u], ss_r, device_id={"seq": to}, device_id_type=MESH
            ).wait_send()
            pltpu.make_async_remote_copy(
                resall.at[0, u], resall.at[0, u], sr_s, sr_r.at[u], device_id={"seq": to}, device_id_type=MESH
            ).wait_recv()

    send_res = across(resall.at[0], resall.at[1], 4)
    send_res.start()
    send_res.wait()

    def weights(blk, hp, hh):
        if blk == 2:
            slot = jnp.where(hp // 2 == core, 0, 1)
            unit0 = 8 + (hp % 2) * 2
        else:
            slot, unit0 = blk, hp * 2
        ra, rb = resall[slot, unit0], resall[slot, unit0 + 1]

        def res(j):
            return jnp.concatenate([ra[3 * hh + j : 3 * hh + j + 1], rb[3 * hh + j : 3 * hh + j + 1]], axis=1)

        s = st[blk, hp]
        m, l, r = (s[3 * hh + j : 3 * hh + j + 1] for j in range(3))
        c = jnp.exp(m - res(0)) * res(1)
        return c, r / l - res(2)

    def totals(which):
        @pl.loop(0, 4)
        def _(hp):
            for blk in range(3):
                parts = []
                for hh in range(2):
                    c, gap = weights(blk, hp, hh)
                    if which == 0:
                        parts.append(c * oab[blk, hp, hh, 0:64, :])
                    else:
                        a, b = oab[blk, hp, hh, 128:192, :], oab[blk, hp, hh, 64:128, :]
                        parts.append((0.125 * c) * (a + gap * b))
                t = jnp.concatenate(parts, axis=0).T
                if blk < 2:
                    obuf[which, blk, 0:16, :, columns(hp)] = t.astype(BF).reshape(16, 16, 128)
                else:
                    own = jnp.where(mine_longer, t, 0.0).astype(BF)
                    their = jnp.where(mine_longer, 0.0, t).astype(BF)
                    obuf[which, 0, 16:32, :, columns(hp)] = own.reshape(16, 16, 128)
                    obuf[which, 1, 16:32, :, columns(hp)] = their.reshape(16, 16, 128)

    def combine(which):
        @pl.loop(0, CHIPS)
        def _(i):
            obuf[which, 0, i] = (obuf[which, 0, i].astype(F32) + sibbuf[which, i].astype(F32)).astype(BF)

    totals(0)
    send_o = across(obuf.at[0, 1], sibbuf.at[0], 5)
    send_o.start()
    totals(1)
    send_dq = across(obuf.at[1, 1], sibbuf.at[1], 6)
    send_dq.start()
    send_o.wait()
    combine(0)
    spread(lambda p: obuf.at[0, 0, p], rsbuf.at[0], rs_s.at[0], rs_r.at[0])
    rsbuf[0, me] = obuf[0, 0, me]
    send_dq.wait()
    combine(1)
    spread(lambda p: obuf.at[1, 0, p], rsbuf.at[1], rs_s.at[1], rs_r.at[1])
    rsbuf[1, me] = obuf[1, 0, me]

    @pl.loop(0, 4)
    def _(hp):
        zero64 = jnp.zeros((64, 512), BF)
        zero256 = jnp.zeros((64, 256), BF)
        outs = []
        for blk in range(3):
            acc = None
            for hh in range(2):
                c, gap = weights(blk, hp, hh)
                qh = qt_s[blk, hp, 64 * hh : 64 * hh + 64, :].astype(F32)
                gh = gt_s[blk, hp, 64 * hh : 64 * hh + 64, :].astype(F32)
                qc = c * qh
                wk = jnp.concatenate([qc.astype(BF), (gap * qc).astype(BF)], axis=1)
                wv = jnp.concatenate([zero256, (c * gh).astype(BF)], axis=1)
                rows = [wk, zero64, wv, zero64] if hh == 0 else [zero64, wk, zero64, wv]
                part = dot_nt(ep[blk, 2 * hp + hh], jnp.concatenate(rows, axis=0))
                acc = part if acc is None else acc + part
            outs.append(acc)
        mine = outs[0] + jnp.where(mine_longer, outs[2], 0.0)
        theirs = outs[1] + jnp.where(mine_longer, 0.0, outs[2])
        dk_ref[core, :, columns(hp)] = mine[:, 0:128].astype(BF)
        dv_ref[core, :, columns(hp)] = mine[:, 128:256].astype(BF)
        dk_ref[other, :, columns(hp)] = theirs[:, 0:128].astype(BF)
        dv_ref[other, :, columns(hp)] = theirs[:, 128:256].astype(BF)

    landed(rsbuf.at[0], rs_s.at[0], rs_r.at[0])
    attended = lax.fori_loop(
        0, CHIPS, lambda i, acc: acc + rsbuf[0, i].astype(F32), jnp.zeros((16, 512), F32)
    )
    crecv[head] = jnp.where(valid, attended, 0.0).astype(BF)
    for j in (1, 2, 3):
        to_head(lambda p: crecv.at[head], crecv, csem, j).start()
    landed(rsbuf.at[1], rs_s.at[1], rs_r.at[1])
    total = lax.fori_loop(
        0, CHIPS, lambda i, acc: acc + rsbuf[1, i].astype(F32), jnp.zeros((16, 512), F32)
    )
    dq_ref[...] = total.astype(BF)
    for j in (1, 2, 3):
        from_head(lambda p: crecv.at[head], crecv, csem, j).wait()
    pick = (
        lax.broadcasted_iota(jnp.int32, (4, 16), 1) == lax.broadcasted_iota(jnp.int32, (4, 16), 0) + 4 * head
    ).astype(BF)
    for p in range(4):
        ctx_ref[:, p * 512 : (p + 1) * 512] = dot(pick, crecv[p]).astype(BF)

    @pl.when(is_owner)
    def _():
        whole = strecv.at[pl.ds(0, PEERS)]
        pltpu.make_async_remote_copy(
            whole, whole, sr_s, ss_r, device_id=sibling, device_id_type=MESH
        ).wait_send()


def local(queries, keys, values, grad_out, pad_counts):
    vmem = pl.BlockSpec(memory_space=pltpu.VMEM)
    dma = pltpu.SemaphoreType.DMA
    return pl.pallas_call(
        kernel,
        out_shape=(
            jax.ShapeDtypeStruct(grad_out.shape, BF),
            jax.ShapeDtypeStruct(queries.shape, BF),
            jax.ShapeDtypeStruct(keys.shape, BF),
            jax.ShapeDtypeStruct(values.shape, BF),
        ),
        in_specs=[pl.BlockSpec(memory_space=pltpu.SMEM)] + [vmem] * 4,
        out_specs=(vmem,) * 4,
        scratch_shapes=[
            pltpu.VMEM((4, 16, 512), BF),
            pltpu.VMEM((4, 16, 512), BF),
            pltpu.VMEM((16, 512), BF),
            pltpu.VMEM((2, CHIPS, 16, 512), BF),
            pltpu.VMEM((2, CHIPS, 16, 512), BF),
            pltpu.VMEM((3, 4, 128, 256), BF),
            pltpu.VMEM((3, 4, 128, 256), BF),
            pltpu.VMEM((2, 8, 144, 512), BF),
            pltpu.VMEM((3, 8, 512, 512), BF),
            pltpu.VMEM((3, 4, 2, 192, 256), F32),
            pltpu.VMEM((3, 4, 8, 256), F32),
            pltpu.VMEM((6, 8, 256), F32),
            pltpu.VMEM((12, 8, 128), F32),
            pltpu.VMEM((CHIPS, 8, 128), F32),
            pltpu.VMEM((2, 12, 8, 128), F32),
            pltpu.VMEM((2, 2, CHIPS, 16, 512), BF),
            pltpu.VMEM((2, CHIPS, 16, 512), BF),
            pltpu.VMEM((2, CHIPS, 16, 512), BF),
            pltpu.VMEM((4, 16, 512), BF),
            dma((8,)),
            dma((2,)),
            dma((2,)),
            dma((7,)),
            dma((7,)),
            dma((12,)),
            dma(()),
            dma(()),
            dma((12,)),
            dma((2,)),
            dma((2,)),
            dma((8,)),
        ],
        compiler_params=pltpu.CompilerParams(
            collective_id=0, has_side_effects=True, vmem_limit_bytes=52 * 2**20
        ),
    )(pad_counts, queries, keys, values, grad_out)


def solution(mesh):
    return jax.shard_map(
        local,
        mesh=mesh,
        in_specs=(
            P(("grp", "seq"), "head"),
            P(None, ("grp", "seq"), "head"),
            P(None, ("grp", "seq"), "head"),
            P(("grp", "seq", "head"), None),
            P(),
        ),
        out_specs=(
            P(("grp", "seq", "head"), None),
            P(("grp", "seq"), "head"),
            P(None, ("grp", "seq"), "head"),
            P(None, ("grp", "seq"), "head"),
        ),
        check_vma=False,
    )
```

```python
import jax
import jax.numpy as jnp
from jax import lax
from jax.experimental import pallas as pl
from jax.experimental.pallas import tpu as pltpu
from jax.sharding import PartitionSpec as P

MESH = pl.DeviceIdType.MESH
CHIPS = 32
PEERS = CHIPS - 1
BF = jnp.bfloat16
F32 = jnp.float32


def peer_of(me, i):
    x, z, y = me // 8, (me // 4) % 2, me % 4
    return ((x + i // 8) % 4) * 8 + ((z + (i // 4) % 2) % 2) * 4 + (y + i % 4) % 4


def dot(a, b):
    return lax.dot_general(a, b, (((1,), (0,)), ((), ())), preferred_element_type=F32)


def dot_nt(a, b):
    return lax.dot_general(a, b, (((1,), (1,)), ((), ())), preferred_element_type=F32)


def columns(hp):
    return pl.ds(pl.multiple_of(hp * 128, 128), 128)


def split3(x):
    a = x.astype(BF).astype(F32)
    b = (x - a).astype(BF).astype(F32)
    return a, b, (x - a - b).astype(BF).astype(F32)


def onehot(shape, rule):
    r = lax.broadcasted_iota(jnp.int32, shape, 0)
    c = lax.broadcasted_iota(jnp.int32, shape, 1)
    return rule(r, c).astype(BF)


def kernel(
    pad_ref, q_ref, k_ref, v_ref, g_ref,
    ctx_ref, dq_ref, dk_ref, dv_ref,
    gsend, grecv, gmine, qall, gall, qt_s, gt_s, vkt, ep, ob, ab,
    st, sd, obsib, absib, stsib, sdsib, cst, comb, rsbuf, wts, own, agbuf, gst, xs, xr, crecv,
    hsem, gat_s, gat_r, sib_s, sib_r, big_s, small_s, rs_r, ag_s, ag_r, csem,
):
    core = lax.axis_index("grp")
    me = lax.axis_index("seq")
    head = lax.axis_index("head")
    other = 1 - core
    sibling = {"grp": other}
    early = me < 16

    barrier = pltpu.get_barrier_semaphore()

    @pl.loop(1, CHIPS)
    def _(i):
        pl.semaphore_signal(barrier, inc=1, device_id={"seq": peer_of(me, i)}, device_id_type=MESH)

    pl.semaphore_signal(barrier, inc=1, device_id=sibling, device_id_type=MESH)
    for j in (1, 2, 3):
        pl.semaphore_signal(barrier, inc=1, device_id={"head": (head + j) % 4}, device_id_type=MESH)

    @pl.loop(0, 8)
    def _(i):
        pair, hp = i // 4, i % 4
        kt = k_ref[pair, :, columns(hp)].T
        vt = v_ref[pair, :, columns(hp)].T
        for hh in range(2):
            vkt[pair, 2 * hp + hh, 0:64, :] = vt[64 * hh : 64 * hh + 64]
            vkt[pair, 2 * hp + hh, 64:128, :] = kt[64 * hh : 64 * hh + 64]
            vkt[pair, 2 * hp + hh, 128:144, :] = jnp.ones((16, 512), BF)

    place = onehot((16, 4), lambda r, c: r == c + 4 * head)
    for p in range(4):
        gsend[p] = dot(place, g_ref[:, p * 512 : (p + 1) * 512]).astype(BF)

    pl.semaphore_wait(barrier, PEERS + 4)

    def to_head(src, dst, sems, j):
        p = (head + j) % 4
        return pltpu.make_async_remote_copy(
            src(p), dst.at[head], sems.at[j], sems.at[4 + head], device_id={"head": p}, device_id_type=MESH
        )

    def from_head(src, dst, sems, j):
        p = (head + j) % 4
        return pltpu.make_async_remote_copy(
            src(p), dst.at[p], sems.at[j], sems.at[4 + p], device_id={"head": p}, device_id_type=MESH
        )

    def pending(ref, send, recv):
        return pltpu.make_async_remote_copy(ref, ref, send, recv, device_id=sibling, device_id_type=MESH)

    def spread(src, dst, send, recv):
        @pl.loop(1, CHIPS)
        def _(i):
            pltpu.make_async_remote_copy(
                src, dst.at[me], send, recv, device_id={"seq": peer_of(me, i)}, device_id_type=MESH
            ).start()

    def landed(dst, send, recv):
        copy = pending(dst.at[pl.ds(0, PEERS)], send, recv)
        copy.wait_recv()
        copy.wait_send()

    def across(src, dst, k):
        return pltpu.make_async_remote_copy(
            src, dst, sib_s.at[k], sib_r.at[k], device_id=sibling, device_id_type=MESH
        )

    for j in (1, 2, 3):
        to_head(lambda p: gsend.at[p], grecv, hsem, j).start()
    spread(q_ref, qall.at[0], gat_s.at[0], gat_r.at[0])
    qall[0, me] = q_ref[...]
    grecv[head] = gsend[head]
    for j in (1, 2, 3):
        from_head(lambda p: gsend.at[p], grecv, hsem, j).wait()

    token = lax.broadcasted_iota(jnp.int32, (16, 512), 0) + me * 16
    gsum = (grecv[0].astype(F32) + grecv[1].astype(F32)) + (grecv[2].astype(F32) + grecv[3].astype(F32))
    gown = jnp.where(token < 512 - pad_ref[core], gsum, 0.0).astype(BF)
    gmine[...] = gown
    spread(gmine, gall.at[0], gat_s.at[1], gat_r.at[1])
    gall[0, me] = gown

    longer = jnp.where(pad_ref[1] < pad_ref[0], 1, 0)
    mine_longer = longer == core
    third_slot = jnp.where(mine_longer, 0, 1)

    row = lax.broadcasted_iota(jnp.int32, (128, 256), 0)

    def only(t, hh):
        return jnp.where((row < 64) if hh == 0 else (row >= 64), t, jnp.zeros((), t.dtype))

    def forward(blk, pair, slot, half):
        @pl.loop(0, 4)
        def _(hp):
            q = qall[slot, half * 16 : half * 16 + 16, :, columns(hp)].reshape(256, 128)
            qt = (q * jnp.asarray(0.125, BF)).T
            qt_s[blk, hp] = qt
            k = k_ref[pair, :, columns(hp)]
            for hh in range(2):
                s = dot(k, only(qt, hh))
                m = jnp.max(s, axis=0, keepdims=True)
                p = jnp.exp(s - m).astype(BF)
                ep[blk, 2 * hp + hh, :, 256:512] = p
                o = dot(vkt[pair, 2 * hp + hh], p)
                ob[blk, hp, 64 * hh : 64 * hh + 64, :] = o[0:64].astype(BF)
                ob[blk, hp, 128 + 64 * hh : 192 + 64 * hh, :] = o[64:128].astype(BF)
                st[blk, 2 * hp + hh, 0:1, :] = m
                st[blk, 2 * hp + hh, 1:2, :] = o[128:129]

    def backward(blk, pair, slot, half):
        @pl.loop(0, 4)
        def _(hp):
            gt = gall[slot, half * 16 : half * 16 + 16, :, columns(hp)].reshape(256, 128).T
            gt_s[blk, hp] = gt
            v = v_ref[pair, :, columns(hp)]
            for hh in range(2):
                dp = dot(v, only(gt, hh))
                o = ob[blk, hp, 64 * hh : 64 * hh + 64, :].astype(F32)
                r = jnp.sum(gt[64 * hh : 64 * hh + 64].astype(F32) * o, axis=0, keepdims=True)
                d = r / st[blk, 2 * hp + hh, 1:2, :]
                e = (ep[blk, 2 * hp + hh, :, 256:512].astype(F32) * (dp - d)).astype(BF)
                ep[blk, 2 * hp + hh, :, 0:256] = e
                a = dot(vkt[pair, 2 * hp + hh, 64:128, :], e)
                ab[blk, hp, 64 * hh : 64 * hh + 64, :] = a.astype(BF)
                sd[blk, 2 * hp + hh, 0:1, :] = d

    def to_owners(which, wide, narrow):
        @pl.loop(1, CHIPS)
        def _(i):
            p = peer_of(me, i)

            @pl.when(p < 16)
            def _():
                pltpu.make_async_remote_copy(
                    comb.at[which, p, :, pl.ds(0, wide)], rsbuf.at[which, me, :, pl.ds(0, wide)],
                    big_s.at[which], rs_r.at[which], device_id={"seq": p}, device_id_type=MESH,
                ).start()

            @pl.when(p >= 16)
            def _():
                pltpu.make_async_remote_copy(
                    comb.at[which, p, :, pl.ds(0, narrow)], rsbuf.at[which, me, :, pl.ds(0, narrow)],
                    small_s.at[which], rs_r.at[which], device_id={"seq": p}, device_id_type=MESH,
                ).start()

        rsbuf[which, me] = comb[which, me]

    def owners_landed(which, wide, narrow):
        @pl.when(early)
        def _():
            pending(rsbuf.at[which, pl.ds(0, 31), :, pl.ds(0, wide)], big_s.at[which], rs_r.at[which]).wait_recv()
            pending(comb.at[which, pl.ds(0, 15), :, pl.ds(0, wide)], big_s.at[which], rs_r.at[which]).wait_send()
            pending(comb.at[which, pl.ds(0, 16), :, pl.ds(0, narrow)], small_s.at[which], rs_r.at[which]).wait_send()

        @pl.when(jnp.logical_not(early))
        def _():
            pending(rsbuf.at[which, pl.ds(0, 31), :, pl.ds(0, narrow)], big_s.at[which], rs_r.at[which]).wait_recv()
            pending(comb.at[which, pl.ds(0, 16), :, pl.ds(0, wide)], big_s.at[which], rs_r.at[which]).wait_send()
            pending(comb.at[which, pl.ds(0, 15), :, pl.ds(0, narrow)], small_s.at[which], rs_r.at[which]).wait_send()

    def place_of(i):
        first = jnp.where(i < 4, 0, 2)
        hp = jnp.where(i < 4, i, 2 * core + i - 4)
        return first, hp, pl.ds(jnp.where(i < 4, 0, 16), 16), columns(jnp.where(i < 4, i, i - 4))

    def combine_forward():
        @pl.loop(0, 6)
        def _(i):
            blk, hp, chips, cols = place_of(i)
            os, bs = [], []
            for hh in range(2):
                a, b = st[blk, 2 * hp + hh], stsib[2 * i + hh]
                m = jnp.maximum(a[0:1], b[0:1])
                wa, wb = jnp.exp(a[0:1] - m), jnp.exp(b[0:1] - m)
                cst[2 * i + hh, 0:1, :] = m
                cst[2 * i + hh, 1:2, :] = wa * a[1:2] + wb * b[1:2]
                cst[2 * i + hh, 2:3, :] = wa
                cst[2 * i + hh, 3:4, :] = wb
                for out, lo in ((os, 64 * hh), (bs, 128 + 64 * hh)):
                    x = ob[blk, hp, lo : lo + 64, :].astype(F32)
                    y = obsib[i, lo : lo + 64, :].astype(F32)
                    out.append(wa * x + wb * y)
            comb[0, chips, :, cols] = jnp.concatenate(os, axis=0).T.astype(BF).reshape(16, 16, 128)
            comb[1, chips, :, cols] = jnp.concatenate(bs, axis=0).T.astype(BF).reshape(16, 16, 128)

        m8, l8 = cst[0:8, 0, :], cst[0:8, 1, :]
        pad = jnp.zeros((128 - 48, 256), F32)
        tile = jnp.concatenate([*split3(m8), *split3(l8), pad], axis=0).T.astype(BF)
        comb[0, 0:16, :, 512:640] = tile.reshape(16, 16, 128)
        none = jnp.zeros((4, 256), F32)
        m8 = jnp.concatenate([cst[8:12, 0, :], none], axis=0)
        l8 = jnp.concatenate([cst[8:12, 1, :], none], axis=0)
        tile = jnp.concatenate([*split3(m8), *split3(l8), pad], axis=0).T.astype(BF)
        comb[0, 16:32, :, 256:384] = tile.reshape(16, 16, 128)

    def combine_backward():
        @pl.loop(0, 6)
        def _(i):
            blk, hp, chips, cols = place_of(i)
            parts = []
            for hh in range(2):
                c = cst[2 * i + hh]
                l, wa, wb = c[1:2], c[2:3], c[3:4]
                da, db = sd[blk, 2 * hp + hh, 0:1, :], sdsib[2 * i + hh, 0:1, :]
                d = (wa * st[blk, 2 * hp + hh, 1:2, :] * da + wb * stsib[2 * i + hh, 1:2, :] * db) / l
                cst[2 * i + hh, 4:5, :] = d
                lo, bo = 64 * hh, 128 + 64 * hh
                xa, xb = ab[blk, hp, lo : lo + 64, :].astype(F32), ob[blk, hp, bo : bo + 64, :].astype(F32)
                ya, yb = absib[i, lo : lo + 64, :].astype(F32), obsib[i, bo : bo + 64, :].astype(F32)
                parts.append(wa * (xa + (da - d) * xb) + wb * (ya + (db - d) * yb))
            comb[2, chips, :, cols] = jnp.concatenate(parts, axis=0).T.astype(BF).reshape(16, 16, 128)

        pad = jnp.zeros((128 - 24, 256), F32)
        tile = jnp.concatenate([*split3(cst[0:8, 4, :]), pad], axis=0).T.astype(BF)
        comb[2, 0:16, :, 512:640] = tile.reshape(16, 16, 128)
        d8 = jnp.concatenate([cst[8:12, 4, :], jnp.zeros((4, 256), F32)], axis=0)
        tile = jnp.concatenate([*split3(d8), pad], axis=0).T.astype(BF)
        comb[2, 16:32, :, 256:384] = tile.reshape(16, 16, 128)

    stat_cols = pl.ds(pl.multiple_of(jnp.where(early, 512, 256), 128), 128)
    width = jnp.where(early, 512, 256)
    inside = lax.broadcasted_iota(jnp.int32, (16, 512), 1) < width

    def expand(first):
        return onehot((128, 512), lambda r, c: (r >= first) & (r < first + 24) & ((r - first) % 8 == c // 64))

    def repeat(first):
        return onehot((128, 128), lambda r, c: (r >= first) & (r < first + 24) & ((r - first) % 8 == c % 8))

    def own_attended():
        s = rsbuf[0, :, :, stat_cols].reshape(512, 128)
        m_all = dot(s, expand(0)).reshape(CHIPS, 16, 512)
        wts[...] = jnp.exp(m_all - jnp.max(m_all, axis=0, keepdims=True))
        l_sum = jnp.sum(wts[...] * dot(s, expand(24)).reshape(CHIPS, 16, 512), axis=0)
        inv = 1.0 / jnp.where(inside, l_sum, 1.0)
        att = jnp.sum(wts[...] * rsbuf[0, :, :, 0:512].astype(F32), axis=0)
        att = jnp.where(inside, att * inv, 0.0)
        third_g = gall[third_slot, me, :, pl.ds(pl.multiple_of(256 * core, 128), 256)]
        third_g = jnp.concatenate([third_g, jnp.zeros((16, 256), BF)], axis=1)
        g = jnp.where(early, gmine[...].astype(F32), third_g.astype(F32))
        prods = split3(g * att)
        same = onehot((512, 512), lambda r, c: r // 64 == c // 64)
        to8 = onehot((512, 128), lambda r, c: r // 64 == c % 8)
        delta = sum(dot(x.astype(BF), same) for x in prods)
        delta8 = sum(dot(x.astype(BF), to8) for x in prods)
        own[0] = inv
        own[1] = delta
        m8 = dot(s, repeat(0)).reshape(CHIPS, 16, 128)
        l8 = dot(s, repeat(24)).reshape(CHIPS, 16, 128)
        top8 = jnp.max(m8, axis=0)
        l8 = jnp.sum(jnp.exp(m8 - top8[None]) * l8, axis=0)
        inv8 = 1.0 / jnp.where(l8 > 0, l8, 1.0)
        lane = lax.broadcasted_iota(jnp.int32, (16, 128), 1) // 8
        tile = jnp.zeros((16, 128), F32)
        for n, term in enumerate((*split3(top8), *split3(inv8), *split3(delta8))):
            tile = jnp.where(lane == n, term, tile)
        agbuf[0, me] = tile.astype(BF)
        spread(agbuf.at[0, me], agbuf.at[0], ag_s, ag_r)
        xs[0] = att.astype(BF)

    def own_queries():
        ds = rsbuf[2, :, :, stat_cols].reshape(512, 128)
        d_all = dot(ds, expand(0)).reshape(CHIPS, 16, 512)
        a = rsbuf[2, :, :, 0:512].astype(F32)
        b = rsbuf[1, :, :, 0:512].astype(F32)
        t = jnp.sum(wts[...] * (a + (d_all - own[1][None]) * b), axis=0)
        xs[1] = jnp.where(inside, t * own[0] * 0.125, 0.0).astype(BF)

    def settle(which):
        @pl.when(jnp.logical_not(early))
        def _():
            swap = across(xs.at[which, :, pl.ds(0, 256)], xr.at[which], 8 + which)
            swap.start()
            swap.wait()
            mine, their = xs[which, :, 0:256].astype(F32), xr[which].astype(F32)
            both = jnp.concatenate(
                [jnp.where(core == 0, mine, their), jnp.where(core == 0, their, mine)], axis=1
            )
            xs[which] = jnp.where(mine_longer, both, 0.0).astype(BF)

    landed(qall.at[0], gat_s.at[0], gat_r.at[0])
    send_q = across(qall.at[0], qall.at[1], 0)
    send_q.start()
    forward(0, core, 0, 0)
    send_q.wait()
    forward(1, other, 1, 0)
    obs_1 = across(ob.at[1], obsib.at[pl.ds(0, 4)], 2)
    st_1 = across(st.at[1], stsib.at[pl.ds(0, 8)], 3)
    obs_1.start()
    st_1.start()
    landed(gall.at[0], gat_s.at[1], gat_r.at[1])
    send_g = across(gall.at[0], gall.at[1], 1)
    send_g.start()
    forward(2, longer, third_slot, 1)
    obs_2 = across(ob.at[2, pl.ds(2 * other, 2)], obsib.at[pl.ds(4, 2)], 4)
    st_2 = across(st.at[2, pl.ds(4 * other, 4)], stsib.at[pl.ds(8, 4)], 5)
    obs_2.start()
    st_2.start()
    send_g.wait()
    obs_1.wait()
    st_1.wait()
    obs_2.wait()
    st_2.wait()
    combine_forward()
    to_owners(0, 640, 384)
    to_owners(1, 512, 256)
    backward(1, other, 1, 0)
    abs_1 = across(ab.at[1], absib.at[pl.ds(0, 4)], 6)
    sd_1 = across(sd.at[1], sdsib.at[pl.ds(0, 8)], 7)
    abs_1.start()
    sd_1.start()
    backward(2, longer, third_slot, 1)
    abs_2 = across(ab.at[2, pl.ds(2 * other, 2)], absib.at[pl.ds(4, 2)], 10)
    sd_2 = across(sd.at[2, pl.ds(4 * other, 4)], sdsib.at[pl.ds(8, 4)], 11)
    abs_2.start()
    sd_2.start()
    owners_landed(0, 640, 384)
    own_attended()
    backward(0, core, 0, 0)
    abs_1.wait()
    sd_1.wait()
    abs_2.wait()
    sd_2.wait()
    combine_backward()
    to_owners(2, 640, 384)

    settle(0)
    third_valid = token < 512 - pad_ref[core]
    crecv[head] = jnp.where(third_valid, xs[0].astype(F32), 0.0).astype(BF)
    for j in (1, 2, 3):
        to_head(lambda p: crecv.at[head], crecv, csem, j).start()

    landed(agbuf.at[0], ag_s, ag_r)
    send_ag = across(agbuf.at[0], agbuf.at[1], 12)
    send_ag.start()
    send_ag.wait()

    for blk in range(3):
        if blk < 2:
            t = agbuf[blk, 0:16].reshape(256, 128).T.astype(F32)
            terms = [t[8 * n : 8 * n + 8] for n in range(9)]
        else:
            t0 = agbuf[core, 16:32].reshape(256, 128).T.astype(F32)
            t1 = agbuf[other, 16:32].reshape(256, 128).T.astype(F32)
            terms = [
                jnp.concatenate([t0[8 * n : 8 * n + 4], t1[8 * n : 8 * n + 4]], axis=0) for n in range(9)
            ]
        top, inv, delta = (terms[n] + terms[n + 1] + terms[n + 2] for n in (0, 3, 6))
        c = jnp.exp(st[blk, :, 0, :] - top) * inv
        gap = sd[blk, :, 0, :] - delta
        for h in range(8):
            gst[blk, h, 0:1, :] = c[h : h + 1]
            gst[blk, h, 1:2, :] = gap[h : h + 1]

    @pl.loop(0, 4)
    def _(hp):
        zero64 = jnp.zeros((64, 512), BF)
        zero256 = jnp.zeros((64, 256), BF)
        outs = []
        for blk in range(3):
            acc = None
            for hh in range(2):
                c, gap = gst[blk, 2 * hp + hh, 0:1, :], gst[blk, 2 * hp + hh, 1:2, :]
                qh = qt_s[blk, hp, 64 * hh : 64 * hh + 64, :].astype(F32)
                gh = gt_s[blk, hp, 64 * hh : 64 * hh + 64, :].astype(F32)
                qc = c * qh
                wk = jnp.concatenate([qc.astype(BF), (gap * qc).astype(BF)], axis=1)
                wv = jnp.concatenate([zero256, (c * gh).astype(BF)], axis=1)
                rows = [wk, zero64, wv, zero64] if hh == 0 else [zero64, wk, zero64, wv]
                part = dot_nt(ep[blk, 2 * hp + hh], jnp.concatenate(rows, axis=0))
                acc = part if acc is None else acc + part
            outs.append(acc)
        mine = outs[0] + jnp.where(mine_longer, outs[2], 0.0)
        theirs = outs[1] + jnp.where(mine_longer, 0.0, outs[2])
        dk_ref[core, :, columns(hp)] = mine[:, 0:128].astype(BF)
        dv_ref[core, :, columns(hp)] = mine[:, 128:256].astype(BF)
        dk_ref[other, :, columns(hp)] = theirs[:, 0:128].astype(BF)
        dv_ref[other, :, columns(hp)] = theirs[:, 128:256].astype(BF)

    for j in (1, 2, 3):
        from_head(lambda p: crecv.at[head], crecv, csem, j).wait()
    pick = onehot((4, 16), lambda r, c: c == r + 4 * head)
    for p in range(4):
        ctx_ref[:, p * 512 : (p + 1) * 512] = dot(pick, crecv[p]).astype(BF)

    owners_landed(1, 512, 256)
    owners_landed(2, 640, 384)
    own_queries()
    settle(1)
    dq_ref[...] = xs[1]


def local(queries, keys, values, grad_out, pad_counts):
    vmem = pl.BlockSpec(memory_space=pltpu.VMEM)
    dma = pltpu.SemaphoreType.DMA
    return pl.pallas_call(
        kernel,
        out_shape=(
            jax.ShapeDtypeStruct(grad_out.shape, BF),
            jax.ShapeDtypeStruct(queries.shape, BF),
            jax.ShapeDtypeStruct(keys.shape, BF),
            jax.ShapeDtypeStruct(values.shape, BF),
        ),
        in_specs=[pl.BlockSpec(memory_space=pltpu.SMEM)] + [vmem] * 4,
        out_specs=(vmem,) * 4,
        scratch_shapes=[
            pltpu.VMEM((4, 16, 512), BF),
            pltpu.VMEM((4, 16, 512), BF),
            pltpu.VMEM((16, 512), BF),
            pltpu.VMEM((2, CHIPS, 16, 512), BF),
            pltpu.VMEM((2, CHIPS, 16, 512), BF),
            pltpu.VMEM((3, 4, 128, 256), BF),
            pltpu.VMEM((3, 4, 128, 256), BF),
            pltpu.VMEM((2, 8, 144, 512), BF),
            pltpu.VMEM((3, 8, 512, 512), BF),
            pltpu.VMEM((3, 4, 256, 256), BF),
            pltpu.VMEM((3, 4, 128, 256), BF),
            pltpu.VMEM((3, 8, 8, 256), F32),
            pltpu.VMEM((3, 8, 8, 256), F32),
            pltpu.VMEM((6, 256, 256), BF),
            pltpu.VMEM((6, 128, 256), BF),
            pltpu.VMEM((12, 8, 256), F32),
            pltpu.VMEM((12, 8, 256), F32),
            pltpu.VMEM((12, 8, 256), F32),
            pltpu.VMEM((3, CHIPS, 16, 640), BF),
            pltpu.VMEM((3, CHIPS, 16, 640), BF),
            pltpu.VMEM((CHIPS, 16, 512), F32),
            pltpu.VMEM((2, 16, 512), F32),
            pltpu.VMEM((2, CHIPS, 16, 128), BF),
            pltpu.VMEM((3, 8, 8, 256), F32),
            pltpu.VMEM((2, 16, 512), BF),
            pltpu.VMEM((2, 16, 256), BF),
            pltpu.VMEM((4, 16, 512), BF),
            dma((8,)),
            dma((2,)),
            dma((2,)),
            dma((13,)),
            dma((13,)),
            dma((3,)),
            dma((3,)),
            dma((3,)),
            dma(()),
            dma(()),
            dma((8,)),
        ],
        compiler_params=pltpu.CompilerParams(
            collective_id=0, has_side_effects=True, vmem_limit_bytes=48 * 2**20
        ),
    )(pad_counts, queries, keys, values, grad_out)


def solution(mesh):
    return jax.shard_map(
        local,
        mesh=mesh,
        in_specs=(
            P(("grp", "seq"), "head"),
            P(None, ("grp", "seq"), "head"),
            P(None, ("grp", "seq"), "head"),
            P(("grp", "seq", "head"), None),
            P(),
        ),
        out_specs=(
            P(("grp", "seq", "head"), None),
            P(("grp", "seq"), "head"),
            P(None, ("grp", "seq"), "head"),
            P(None, ("grp", "seq"), "head"),
        ),
        check_vma=False,
    )
```

```python
import jax
import jax.numpy as jnp
from jax import lax
from jax.experimental import pallas as pl
from jax.experimental.pallas import tpu as pltpu
from jax.sharding import PartitionSpec as P

MESH = pl.DeviceIdType.MESH
CHIPS = 32
PEERS = CHIPS - 1
BF = jnp.bfloat16
F32 = jnp.float32


def peer_of(me, i):
    x, z, y = me // 8, (me // 4) % 2, me % 4
    return ((x + i // 8) % 4) * 8 + ((z + (i // 4) % 2) % 2) * 4 + (y + i % 4) % 4


def dot(a, b):
    return lax.dot_general(a, b, (((1,), (0,)), ((), ())), preferred_element_type=F32)


def dot_nt(a, b):
    return lax.dot_general(a, b, (((1,), (1,)), ((), ())), preferred_element_type=F32)


def columns(hp):
    return pl.ds(pl.multiple_of(hp * 128, 128), 128)


def split3(x):
    a = x.astype(BF).astype(F32)
    b = (x - a).astype(BF).astype(F32)
    return a, b, (x - a - b).astype(BF).astype(F32)


def onehot(shape, rule):
    r = lax.broadcasted_iota(jnp.int32, shape, 0)
    c = lax.broadcasted_iota(jnp.int32, shape, 1)
    return rule(r, c).astype(BF)


def kernel(
    pad_ref, q_hbm, k_hbm, v_hbm, g_hbm,
    ctx_ref, dq_ref, dk_ref, dv_ref,
    q_ref, k_ref, v_ref, g_ref,
    gsend, grecv, gmine, qall, gall, qt_s, gt_s, vkt, ep, ob, ab,
    st, sd, obsib, absib, stsib, sdsib, cst, oc, sbuf, comb, rsbuf, wts, own, ddev, agbuf, gst, xs, xr, crecv,
    lsem, hsem, gat_s, gat_r, sib_s, sib_r, big_s, small_s, rs_r, ag_s, ag_r, csem,
):
    core = lax.axis_index("grp")
    me = lax.axis_index("seq")
    head = lax.axis_index("head")
    other = 1 - core
    sibling = {"grp": other}
    early = me < 16

    barrier = pltpu.get_barrier_semaphore()

    @pl.loop(1, CHIPS)
    def _(i):
        pl.semaphore_signal(barrier, inc=1, device_id={"seq": peer_of(me, i)}, device_id_type=MESH)

    pl.semaphore_signal(barrier, inc=1, device_id=sibling, device_id_type=MESH)
    for j in (1, 2, 3):
        pl.semaphore_signal(barrier, inc=1, device_id={"head": (head + j) % 4}, device_id_type=MESH)

    loads = [
        pltpu.make_async_copy(src, dst, lsem.at[n])
        for n, (src, dst) in enumerate(((g_hbm, g_ref), (q_hbm, q_ref), (k_hbm, k_ref), (v_hbm, v_ref)))
    ]
    for load in loads:
        load.start()
    for load in loads:
        load.wait()

    @pl.loop(0, 8)
    def _(i):
        pair, hp = i // 4, i % 4
        kt = k_ref[pair, :, columns(hp)].T
        vt = v_ref[pair, :, columns(hp)].T
        for hh in range(2):
            vkt[pair, 2 * hp + hh, 0:64, :] = vt[64 * hh : 64 * hh + 64]
            vkt[pair, 2 * hp + hh, 64:128, :] = kt[64 * hh : 64 * hh + 64]
            vkt[pair, 2 * hp + hh, 128:144, :] = jnp.ones((16, 512), BF)

    place = onehot((16, 4), lambda r, c: r == c + 4 * head)
    for p in range(4):
        gsend[p] = dot(place, g_ref[:, p * 512 : (p + 1) * 512]).astype(BF)

    pl.semaphore_wait(barrier, PEERS + 4)

    def to_head(src, dst, sems, j):
        p = (head + j) % 4
        return pltpu.make_async_remote_copy(
            src(p), dst.at[head], sems.at[j], sems.at[4 + head], device_id={"head": p}, device_id_type=MESH
        )

    def from_head(src, dst, sems, j):
        p = (head + j) % 4
        return pltpu.make_async_remote_copy(
            src(p), dst.at[p], sems.at[j], sems.at[4 + p], device_id={"head": p}, device_id_type=MESH
        )

    def pending(ref, send, recv):
        return pltpu.make_async_remote_copy(ref, ref, send, recv, device_id=sibling, device_id_type=MESH)

    def spread(src, dst, send, recv):
        @pl.loop(1, CHIPS)
        def _(i):
            pltpu.make_async_remote_copy(
                src, dst.at[me], send, recv, device_id={"seq": peer_of(me, i)}, device_id_type=MESH
            ).start()

    def landed(dst, send, recv):
        copy = pending(dst.at[pl.ds(0, PEERS)], send, recv)
        copy.wait_recv()
        copy.wait_send()

    def across(src, dst, k):
        return pltpu.make_async_remote_copy(
            src, dst, sib_s.at[k], sib_r.at[k], device_id=sibling, device_id_type=MESH
        )

    for j in (1, 2, 3):
        to_head(lambda p: gsend.at[p], grecv, hsem, j).start()
    spread(q_ref, qall.at[0], gat_s.at[0], gat_r.at[0])
    qall[0, me] = q_ref[...]
    grecv[head] = gsend[head]
    for j in (1, 2, 3):
        from_head(lambda p: gsend.at[p], grecv, hsem, j).wait()

    token = lax.broadcasted_iota(jnp.int32, (16, 512), 0) + me * 16
    gsum = (grecv[0].astype(F32) + grecv[1].astype(F32)) + (grecv[2].astype(F32) + grecv[3].astype(F32))
    gown = jnp.where(token < 512 - pad_ref[core], gsum, 0.0).astype(BF)
    gmine[...] = gown
    spread(gmine, gall.at[0], gat_s.at[1], gat_r.at[1])
    gall[0, me] = gown

    longer = jnp.where(pad_ref[1] < pad_ref[0], 1, 0)
    mine_longer = longer == core
    third_slot = jnp.where(mine_longer, 0, 1)

    row = lax.broadcasted_iota(jnp.int32, (128, 256), 0)

    def only(t, hh):
        return jnp.where((row < 64) if hh == 0 else (row >= 64), t, jnp.zeros((), t.dtype))

    def pair_of(blk):
        return jnp.where(blk == 0, core, jnp.where(blk == 1, other, longer))

    def tokens_of(buf, slot, blk, hp):
        return buf[slot, pl.ds(16 * (blk // 2), 16), :, columns(hp)].reshape(256, 128).T

    def scores(i):
        blk, hp = i // 4, i % 4
        qt = tokens_of(qall, blk, blk, hp) * jnp.asarray(0.125, BF)
        qt_s[blk, hp] = qt
        k = k_ref[pair_of(blk), :, columns(hp)]
        for hh in range(2):
            sbuf[i % 2, hh] = dot(k, only(qt, hh))

    def forward(i):
        blk, hp = i // 4, i % 4
        pair = pair_of(blk)
        now = [sbuf[i % 2, hh] for hh in range(2)]
        scores(jnp.minimum(i + 1, 11))
        for hh in range(2):
            m = jnp.max(now[hh], axis=0, keepdims=True)
            p = jnp.exp(now[hh] - m).astype(BF)
            ep[blk, 2 * hp + hh, :, 256:512] = p
            o = dot(vkt[pair, 2 * hp + hh], p)
            ob[blk, hp, 64 * hh : 64 * hh + 64, :] = o[0:64].astype(BF)
            ob[blk, hp, 128 + 64 * hh : 192 + 64 * hh, :] = o[64:128].astype(BF)
            st[blk, 2 * hp + hh, 0:1, :] = m
            st[blk, 2 * hp + hh, 1:2, :] = o[128:129]

    def backward(i):
        blk, hp = (i // 4 + 1) % 3, i % 4
        pair = pair_of(blk)
        gt = tokens_of(gall, jnp.where(blk == 2, third_slot, blk), blk, hp)
        gt_s[blk, hp] = gt
        v = v_ref[pair, :, columns(hp)]
        dps = [dot(v, only(gt, hh)) for hh in range(2)]
        for hh in range(2):
            o = ob[blk, hp, 64 * hh : 64 * hh + 64, :].astype(F32)
            r = jnp.sum(gt[64 * hh : 64 * hh + 64].astype(F32) * o, axis=0, keepdims=True)
            d = r / st[blk, 2 * hp + hh, 1:2, :]
            e = (ep[blk, 2 * hp + hh, :, 256:512].astype(F32) * (dps[hh] - d)).astype(BF)
            ep[blk, 2 * hp + hh, :, 0:256] = e
            a = dot(vkt[pair, 2 * hp + hh, 64:128, :], e)
            ab[blk, hp, 64 * hh : 64 * hh + 64, :] = a.astype(BF)
            sd[blk, 2 * hp + hh, 0:1, :] = d

    def to_owners(which, wide, narrow, halves=(0, 1)):
        @pl.loop(1, CHIPS)
        def _(i):
            p = peer_of(me, i)
            for half, cols, sems in ((0, wide, big_s), (1, narrow, small_s)):
                if half in halves:

                    @pl.when(p // 16 == half)
                    def _():
                        pltpu.make_async_remote_copy(
                            comb.at[which, p, :, pl.ds(0, cols)], rsbuf.at[which, me, :, pl.ds(0, cols)],
                            sems.at[which], rs_r.at[which], device_id={"seq": p}, device_id_type=MESH,
                        ).start()

        for half in halves:

            @pl.when(me // 16 == half)
            def _():
                rsbuf[which, me] = comb[which, me]

    def owners_landed(which, wide, narrow):
        @pl.when(early)
        def _():
            pending(rsbuf.at[which, pl.ds(0, 31), :, pl.ds(0, wide)], big_s.at[which], rs_r.at[which]).wait_recv()
            pending(comb.at[which, pl.ds(0, 15), :, pl.ds(0, wide)], big_s.at[which], rs_r.at[which]).wait_send()
            pending(comb.at[which, pl.ds(0, 16), :, pl.ds(0, narrow)], small_s.at[which], rs_r.at[which]).wait_send()

        @pl.when(jnp.logical_not(early))
        def _():
            pending(rsbuf.at[which, pl.ds(0, 31), :, pl.ds(0, narrow)], big_s.at[which], rs_r.at[which]).wait_recv()
            pending(comb.at[which, pl.ds(0, 16), :, pl.ds(0, wide)], big_s.at[which], rs_r.at[which]).wait_send()
            pending(comb.at[which, pl.ds(0, 15), :, pl.ds(0, narrow)], small_s.at[which], rs_r.at[which]).wait_send()

    def place_of(i):
        first = jnp.where(i < 4, 0, 2)
        hp = jnp.where(i < 4, i, 2 * core + i - 4)
        return first, hp, pl.ds(jnp.where(i < 4, 0, 16), 16), columns(jnp.where(i < 4, i, i - 4))

    def combine_forward(first, last):
        @pl.loop(first, last)
        def _(i):
            blk, hp, chips, cols = place_of(i)
            os, bs = [], []
            for hh in range(2):
                a, b = st[blk, 2 * hp + hh], stsib[2 * i + hh]
                m = jnp.maximum(a[0:1], b[0:1])
                wa, wb = jnp.exp(a[0:1] - m), jnp.exp(b[0:1] - m)
                cst[2 * i + hh, 0:1, :] = m
                cst[2 * i + hh, 1:2, :] = wa * a[1:2] + wb * b[1:2]
                cst[2 * i + hh, 2:3, :] = wa
                cst[2 * i + hh, 3:4, :] = wb
                for out, lo in ((os, 64 * hh), (bs, 128 + 64 * hh)):
                    x = ob[blk, hp, lo : lo + 64, :].astype(F32)
                    y = obsib[i, lo : lo + 64, :].astype(F32)
                    out.append(wa * x + wb * y)
            oc[i] = jnp.concatenate(os, axis=0).astype(BF)
            comb[0, chips, :, cols] = oc[i].T.reshape(16, 16, 128)
            comb[1, chips, :, cols] = jnp.concatenate(bs, axis=0).T.astype(BF).reshape(16, 16, 128)

        if first == 0:
            m8, l8 = cst[0:8, 0, :], cst[0:8, 1, :]
        else:
            none = jnp.zeros((4, 256), F32)
            m8 = jnp.concatenate([cst[8:12, 0, :], none], axis=0)
            l8 = jnp.concatenate([cst[8:12, 1, :], none], axis=0)
        pad = jnp.zeros((128 - 48, 256), F32)
        tile = jnp.concatenate([*split3(m8), *split3(l8), pad], axis=0).T.astype(BF).reshape(16, 16, 128)
        if first == 0:
            comb[0, 0:16, :, 512:640] = tile
        else:
            comb[0, 16:32, :, 256:384] = tile

    def combine_backward():
        @pl.loop(0, 6)
        def _(i):
            blk, hp, chips, cols = place_of(i)
            parts = []
            for hh in range(2):
                c = cst[2 * i + hh]
                l, wa, wb = c[1:2], c[2:3], c[3:4]
                da, db = sd[blk, 2 * hp + hh, 0:1, :], sdsib[2 * i + hh, 0:1, :]
                lo, bo = 64 * hh, 128 + 64 * hh
                gt = gt_s[blk, hp, lo : lo + 64, :].astype(F32)
                d = jnp.sum(gt * oc[i, lo : lo + 64, :].astype(F32), axis=0, keepdims=True) / l
                xa, xb = ab[blk, hp, lo : lo + 64, :].astype(F32), ob[blk, hp, bo : bo + 64, :].astype(F32)
                ya, yb = absib[i, lo : lo + 64, :].astype(F32), obsib[i, bo : bo + 64, :].astype(F32)
                parts.append(wa * (xa + (da - d) * xb) + wb * (ya + (db - d) * yb))
            comb[2, chips, :, cols] = jnp.concatenate(parts, axis=0).astype(BF).T.reshape(16, 16, 128)

    stat_cols = pl.ds(pl.multiple_of(jnp.where(early, 512, 256), 128), 128)
    width = jnp.where(early, 512, 256)
    inside = lax.broadcasted_iota(jnp.int32, (16, 512), 1) < width

    def expand(first):
        return onehot((128, 512), lambda r, c: (r >= first) & (r < first + 24) & ((r - first) % 8 == c // 64))

    def repeat(first):
        return onehot((128, 128), lambda r, c: (r >= first) & (r < first + 24) & ((r - first) % 8 == c % 8))

    def own_attended():
        s = rsbuf[0, :, :, stat_cols].reshape(512, 128)
        m_all = dot(s, expand(0)).reshape(CHIPS, 16, 512)
        wts[...] = jnp.exp(m_all - jnp.max(m_all, axis=0, keepdims=True))
        l_all = dot(s, expand(24)).reshape(CHIPS, 16, 512)
        l_sum = jnp.sum(wts[...] * l_all, axis=0)
        inv = 1.0 / jnp.where(inside, l_sum, 1.0)
        att = jnp.sum(wts[...] * rsbuf[0, :, :, 0:512].astype(F32), axis=0)
        att = jnp.where(inside, att * inv, 0.0)
        third_g = gall[third_slot, me, :, pl.ds(pl.multiple_of(256 * core, 128), 256)]
        third_g = jnp.concatenate([third_g, jnp.zeros((16, 256), BF)], axis=1)
        g = jnp.where(early, gmine[...].astype(F32), third_g.astype(F32))
        dprod = jnp.where(inside[None], rsbuf[0, :, :, 0:512].astype(F32) * g[None], 0.0).reshape(512, 512)
        high = dprod.astype(BF)
        low = (dprod - high.astype(F32)).astype(BF)
        prods = split3(g * att)
        same = onehot((512, 512), lambda r, c: r // 64 == c // 64)
        to8 = onehot((512, 128), lambda r, c: r // 64 == c % 8)
        delta = sum(dot(x.astype(BF), same) for x in prods)
        d_dev = (dot(high, same) + dot(low, same)).reshape(CHIPS, 16, 512)
        ddev[...] = d_dev / jnp.where(inside[None], l_all, 1.0) - delta[None]
        delta8 = sum(dot(x.astype(BF), to8) for x in prods)
        own[...] = inv
        m8 = dot(s, repeat(0)).reshape(CHIPS, 16, 128)
        l8 = dot(s, repeat(24)).reshape(CHIPS, 16, 128)
        top8 = jnp.max(m8, axis=0)
        l8 = jnp.sum(jnp.exp(m8 - top8[None]) * l8, axis=0)
        inv8 = 1.0 / jnp.where(l8 > 0, l8, 1.0)
        lane = lax.broadcasted_iota(jnp.int32, (16, 128), 1) // 8
        tile = jnp.zeros((16, 128), F32)
        for n, term in enumerate((*split3(top8), *split3(inv8), *split3(delta8))):
            tile = jnp.where(lane == n, term, tile)
        agbuf[0, me] = tile.astype(BF)
        spread(agbuf.at[0, me], agbuf.at[0], ag_s, ag_r)
        xs[0] = att.astype(BF)

    def own_queries():
        a = rsbuf[2, :, :, 0:512].astype(F32)
        b = rsbuf[1, :, :, 0:512].astype(F32)
        t = jnp.sum(wts[...] * (a + ddev[...] * b), axis=0)
        xs[1] = jnp.where(inside, t * own[...] * 0.125, 0.0).astype(BF)

    def settle(which):
        @pl.when(jnp.logical_not(early))
        def _():
            swap = across(xs.at[which, :, pl.ds(0, 256)], xr.at[which], 8 + which)
            swap.start()
            swap.wait()
            mine, their = xs[which, :, 0:256].astype(F32), xr[which].astype(F32)
            both = jnp.concatenate(
                [jnp.where(core == 0, mine, their), jnp.where(core == 0, their, mine)], axis=1
            )
            xs[which] = jnp.where(mine_longer, both, 0.0).astype(BF)

    send_q = across(qall.at[0], qall.at[1], 0)
    send_g = across(gall.at[0], gall.at[1], 1)
    obs_1 = across(ob.at[1], obsib.at[pl.ds(0, 4)], 2)
    st_1 = across(st.at[1], stsib.at[pl.ds(0, 8)], 3)
    obs_2 = across(ob.at[2, pl.ds(2 * other, 2)], obsib.at[pl.ds(4, 2)], 4)
    st_2 = across(st.at[2, pl.ds(4 * other, 4)], stsib.at[pl.ds(8, 4)], 5)
    abs_1 = across(ab.at[1], absib.at[pl.ds(0, 4)], 6)
    sd_1 = across(sd.at[1], sdsib.at[pl.ds(0, 8)], 7)
    abs_2 = across(ab.at[2, pl.ds(2 * other, 2)], absib.at[pl.ds(4, 2)], 10)
    sd_2 = across(sd.at[2, pl.ds(4 * other, 4)], sdsib.at[pl.ds(8, 4)], 11)

    landed(qall.at[0], gat_s.at[0], gat_r.at[0])
    send_q.start()
    scores(0)

    @pl.loop(0, 12)
    def _(i):
        @pl.when(i == 3)
        def _():
            send_q.wait()

            @pl.loop(16, CHIPS)
            def _(chip):
                qall[2, chip] = jnp.where(mine_longer, qall[0, chip], qall[1, chip])

        forward(i)

        @pl.when(i == 7)
        def _():
            obs_1.start()
            st_1.start()

    obs_2.start()
    st_2.start()
    obs_1.wait()
    st_1.wait()
    combine_forward(0, 4)
    to_owners(0, 640, 384, (0,))
    obs_2.wait()
    st_2.wait()
    combine_forward(4, 6)
    to_owners(0, 640, 384, (1,))
    landed(gall.at[0], gat_s.at[1], gat_r.at[1])
    send_g.start()
    send_g.wait()

    @pl.loop(0, 12)
    def _(i):
        backward(i)

        @pl.when(i == 3)
        def _():
            abs_1.start()
            sd_1.start()

        @pl.when(i == 7)
        def _():
            abs_2.start()
            sd_2.start()
            to_owners(1, 512, 256)

    owners_landed(0, 640, 384)
    own_attended()
    abs_1.wait()
    sd_1.wait()
    abs_2.wait()
    sd_2.wait()
    combine_backward()
    to_owners(2, 512, 256)

    settle(0)
    third_valid = token < 512 - pad_ref[core]
    crecv[head] = jnp.where(third_valid, xs[0].astype(F32), 0.0).astype(BF)
    for j in (1, 2, 3):
        to_head(lambda p: crecv.at[head], crecv, csem, j).start()

    landed(agbuf.at[0], ag_s, ag_r)
    send_ag = across(agbuf.at[0], agbuf.at[1], 12)
    send_ag.start()
    send_ag.wait()

    for blk in range(3):
        if blk < 2:
            t = agbuf[blk, 0:16].reshape(256, 128).T.astype(F32)
            terms = [t[8 * n : 8 * n + 8] for n in range(9)]
        else:
            t0 = agbuf[core, 16:32].reshape(256, 128).T.astype(F32)
            t1 = agbuf[other, 16:32].reshape(256, 128).T.astype(F32)
            terms = [
                jnp.concatenate([t0[8 * n : 8 * n + 4], t1[8 * n : 8 * n + 4]], axis=0) for n in range(9)
            ]
        top, inv, delta = (terms[n] + terms[n + 1] + terms[n + 2] for n in (0, 3, 6))
        c = jnp.exp(st[blk, :, 0, :] - top) * inv
        gap = sd[blk, :, 0, :] - delta
        for h in range(8):
            gst[blk, h, 0:1, :] = c[h : h + 1]
            gst[blk, h, 1:2, :] = gap[h : h + 1]

    @pl.loop(0, 4)
    def _(hp):
        zero64 = jnp.zeros((64, 512), BF)
        zero256 = jnp.zeros((64, 256), BF)
        outs = []
        for blk in range(3):
            acc = None
            for hh in range(2):
                c, gap = gst[blk, 2 * hp + hh, 0:1, :], gst[blk, 2 * hp + hh, 1:2, :]
                qh = qt_s[blk, hp, 64 * hh : 64 * hh + 64, :].astype(F32)
                gh = gt_s[blk, hp, 64 * hh : 64 * hh + 64, :].astype(F32)
                qc = c * qh
                wk = jnp.concatenate([qc.astype(BF), (gap * qc).astype(BF)], axis=1)
                wv = jnp.concatenate([zero256, (c * gh).astype(BF)], axis=1)
                rows = [wk, zero64, wv, zero64] if hh == 0 else [zero64, wk, zero64, wv]
                part = dot_nt(ep[blk, 2 * hp + hh], jnp.concatenate(rows, axis=0))
                acc = part if acc is None else acc + part
            outs.append(acc)
        mine = outs[0] + jnp.where(mine_longer, outs[2], 0.0)
        theirs = outs[1] + jnp.where(mine_longer, 0.0, outs[2])
        dk_ref[core, :, columns(hp)] = mine[:, 0:128].astype(BF)
        dv_ref[core, :, columns(hp)] = mine[:, 128:256].astype(BF)
        dk_ref[other, :, columns(hp)] = theirs[:, 0:128].astype(BF)
        dv_ref[other, :, columns(hp)] = theirs[:, 128:256].astype(BF)

    for j in (1, 2, 3):
        from_head(lambda p: crecv.at[head], crecv, csem, j).wait()
    pick = onehot((4, 16), lambda r, c: c == r + 4 * head)
    for p in range(4):
        ctx_ref[:, p * 512 : (p + 1) * 512] = dot(pick, crecv[p]).astype(BF)

    owners_landed(1, 512, 256)
    owners_landed(2, 512, 256)
    own_queries()
    settle(1)
    dq_ref[...] = xs[1]


def local(queries, keys, values, grad_out, pad_counts):
    vmem = pl.BlockSpec(memory_space=pltpu.VMEM)
    dma = pltpu.SemaphoreType.DMA
    return pl.pallas_call(
        kernel,
        out_shape=(
            jax.ShapeDtypeStruct(grad_out.shape, BF),
            jax.ShapeDtypeStruct(queries.shape, BF),
            jax.ShapeDtypeStruct(keys.shape, BF),
            jax.ShapeDtypeStruct(values.shape, BF),
        ),
        in_specs=[pl.BlockSpec(memory_space=pltpu.SMEM)] + [pl.BlockSpec(memory_space=pl.ANY)] * 4,
        out_specs=(vmem,) * 4,
        scratch_shapes=[
            pltpu.VMEM(queries.shape, BF),
            pltpu.VMEM(keys.shape, BF),
            pltpu.VMEM(values.shape, BF),
            pltpu.VMEM(grad_out.shape, BF),
            pltpu.VMEM((4, 16, 512), BF),
            pltpu.VMEM((4, 16, 512), BF),
            pltpu.VMEM((16, 512), BF),
            pltpu.VMEM((3, CHIPS, 16, 512), BF),
            pltpu.VMEM((2, CHIPS, 16, 512), BF),
            pltpu.VMEM((3, 4, 128, 256), BF),
            pltpu.VMEM((3, 4, 128, 256), BF),
            pltpu.VMEM((2, 8, 144, 512), BF),
            pltpu.VMEM((3, 8, 512, 512), BF),
            pltpu.VMEM((3, 4, 256, 256), BF),
            pltpu.VMEM((3, 4, 128, 256), BF),
            pltpu.VMEM((3, 8, 8, 256), F32),
            pltpu.VMEM((3, 8, 8, 256), F32),
            pltpu.VMEM((6, 256, 256), BF),
            pltpu.VMEM((6, 128, 256), BF),
            pltpu.VMEM((12, 8, 256), F32),
            pltpu.VMEM((12, 8, 256), F32),
            pltpu.VMEM((12, 8, 256), F32),
            pltpu.VMEM((6, 128, 256), BF),
            pltpu.VMEM((2, 2, 512, 256), F32),
            pltpu.VMEM((3, CHIPS, 16, 640), BF),
            pltpu.VMEM((3, CHIPS, 16, 640), BF),
            pltpu.VMEM((CHIPS, 16, 512), F32),
            pltpu.VMEM((16, 512), F32),
            pltpu.VMEM((CHIPS, 16, 512), F32),
            pltpu.VMEM((2, CHIPS, 16, 128), BF),
            pltpu.VMEM((3, 8, 8, 256), F32),
            pltpu.VMEM((2, 16, 512), BF),
            pltpu.VMEM((2, 16, 256), BF),
            pltpu.VMEM((4, 16, 512), BF),
            dma((4,)),
            dma((8,)),
            dma((2,)),
            dma((2,)),
            dma((13,)),
            dma((13,)),
            dma((3,)),
            dma((3,)),
            dma((3,)),
            dma(()),
            dma(()),
            dma((8,)),
        ],
        compiler_params=pltpu.CompilerParams(
            collective_id=0, has_side_effects=True, vmem_limit_bytes=48 * 2**20
        ),
    )(pad_counts, queries, keys, values, grad_out)


def solution(mesh):
    return jax.shard_map(
        local,
        mesh=mesh,
        in_specs=(
            P(("grp", "seq"), "head"),
            P(None, ("grp", "seq"), "head"),
            P(None, ("grp", "seq"), "head"),
            P(("grp", "seq", "head"), None),
            P(),
        ),
        out_specs=(
            P(("grp", "seq", "head"), None),
            P(("grp", "seq"), "head"),
            P(None, ("grp", "seq"), "head"),
            P(None, ("grp", "seq"), "head"),
        ),
        check_vma=False,
    )
```

```python
import jax
import jax.numpy as jnp
from jax import lax
from jax.experimental import pallas as pl
from jax.experimental.pallas import tpu as pltpu
from jax.sharding import PartitionSpec as P

MESH = pl.DeviceIdType.MESH
CHIPS = 32
PEERS = CHIPS - 1
BF = jnp.bfloat16
F32 = jnp.float32


def peer_of(me, i):
    i = 32 - i
    x, z, y = me // 8, (me // 4) % 2, me % 4
    return ((x + i // 8) % 4) * 8 + ((z + (i // 4) % 2) % 2) * 4 + (y + i % 4) % 4


def dot(a, b):
    return lax.dot_general(a, b, (((1,), (0,)), ((), ())), preferred_element_type=F32)


def dot_nt(a, b):
    return lax.dot_general(a, b, (((1,), (1,)), ((), ())), preferred_element_type=F32)


def columns(hp):
    return pl.ds(pl.multiple_of(hp * 128, 128), 128)


def split3(x):
    a = x.astype(BF).astype(F32)
    b = (x - a).astype(BF).astype(F32)
    return a, b, (x - a - b).astype(BF).astype(F32)


def onehot(shape, rule):
    r = lax.broadcasted_iota(jnp.int32, shape, 0)
    c = lax.broadcasted_iota(jnp.int32, shape, 1)
    return rule(r, c).astype(BF)


def kernel(
    pad_ref, q_hbm, k_hbm, v_hbm, g_hbm,
    ctx_ref, dq_ref, dk_ref, dv_ref,
    q_ref, k_ref, v_ref, g_ref,
    gsend, grecv, gmine, qall, gall, qt_s, gt_s, vkt, ep, ob, ab,
    st, sd, obsib, absib, stsib, sdsib, cst, oc, sbuf, comb, rsbuf, wts, own, ddev, agbuf, gst, xs, xr, crecv,
    lsem, hsem, gat_s, gat_r, sib_s, sib_r, big_s, small_s, rs_r, ag_s, ag_r, csem,
):
    core = lax.axis_index("grp")
    me = lax.axis_index("seq")
    head = lax.axis_index("head")
    other = 1 - core
    sibling = {"grp": other}
    early = me < 16

    barrier = pltpu.get_barrier_semaphore()

    @pl.loop(1, CHIPS)
    def _(i):
        pl.semaphore_signal(barrier, inc=1, device_id={"seq": peer_of(me, i)}, device_id_type=MESH)

    pl.semaphore_signal(barrier, inc=1, device_id=sibling, device_id_type=MESH)
    for j in (1, 2, 3):
        pl.semaphore_signal(barrier, inc=1, device_id={"head": (head + j) % 4}, device_id_type=MESH)

    loads = [
        pltpu.make_async_copy(src, dst, lsem.at[n])
        for n, (src, dst) in enumerate(((g_hbm, g_ref), (q_hbm, q_ref), (k_hbm, k_ref), (v_hbm, v_ref)))
    ]
    for load in loads:
        load.start()
    for load in loads:
        load.wait()

    @pl.loop(0, 8)
    def _(i):
        pair, hp = i // 4, i % 4
        kt = k_ref[pair, :, columns(hp)].T
        vt = v_ref[pair, :, columns(hp)].T
        for hh in range(2):
            vkt[pair, 2 * hp + hh, 0:64, :] = vt[64 * hh : 64 * hh + 64]
            vkt[pair, 2 * hp + hh, 64:128, :] = kt[64 * hh : 64 * hh + 64]
            vkt[pair, 2 * hp + hh, 128:144, :] = jnp.ones((16, 512), BF)

    place = onehot((16, 4), lambda r, c: r == c + 4 * head)
    for p in range(4):
        gsend[p] = dot(place, g_ref[:, p * 512 : (p + 1) * 512]).astype(BF)

    pl.semaphore_wait(barrier, PEERS + 4)

    def to_head(src, dst, sems, j):
        p = (head + j) % 4
        return pltpu.make_async_remote_copy(
            src(p), dst.at[head], sems.at[j], sems.at[4 + head], device_id={"head": p}, device_id_type=MESH
        )

    def from_head(src, dst, sems, j):
        p = (head + j) % 4
        return pltpu.make_async_remote_copy(
            src(p), dst.at[p], sems.at[j], sems.at[4 + p], device_id={"head": p}, device_id_type=MESH
        )

    def pending(ref, send, recv):
        return pltpu.make_async_remote_copy(ref, ref, send, recv, device_id=sibling, device_id_type=MESH)

    def spread(src, dst, send, recv):
        @pl.loop(1, CHIPS)
        def _(i):
            pltpu.make_async_remote_copy(
                src, dst.at[me], send, recv, device_id={"seq": peer_of(me, i)}, device_id_type=MESH
            ).start()

    def landed(dst, send, recv):
        copy = pending(dst.at[pl.ds(0, PEERS)], send, recv)
        copy.wait_recv()
        copy.wait_send()

    def across(src, dst, k):
        return pltpu.make_async_remote_copy(
            src, dst, sib_s.at[k], sib_r.at[k], device_id=sibling, device_id_type=MESH
        )

    for j in (1, 2, 3):
        to_head(lambda p: gsend.at[p], grecv, hsem, j).start()
    spread(q_ref, qall.at[0], gat_s.at[0], gat_r.at[0])
    qall[0, me] = q_ref[...]
    grecv[head] = gsend[head]
    for j in (1, 2, 3):
        from_head(lambda p: gsend.at[p], grecv, hsem, j).wait()

    token = lax.broadcasted_iota(jnp.int32, (16, 512), 0) + me * 16
    gsum = (grecv[0].astype(F32) + grecv[1].astype(F32)) + (grecv[2].astype(F32) + grecv[3].astype(F32))
    gown = jnp.where(token < 512 - pad_ref[core], gsum, 0.0).astype(BF)
    gmine[...] = gown
    spread(gmine, gall.at[0], gat_s.at[1], gat_r.at[1])
    gall[0, me] = gown

    longer = jnp.where(pad_ref[1] < pad_ref[0], 1, 0)
    mine_longer = longer == core
    third_slot = jnp.where(mine_longer, 0, 1)

    row = lax.broadcasted_iota(jnp.int32, (128, 256), 0)

    def only(t, hh):
        return jnp.where((row < 64) if hh == 0 else (row >= 64), t, jnp.zeros((), t.dtype))

    def pair_of(blk):
        return jnp.where(blk == 0, core, jnp.where(blk == 1, other, longer))

    def tokens_of(buf, slot, blk, hp):
        return buf[slot, pl.ds(16 * (blk // 2), 16), :, columns(hp)].reshape(256, 128).T

    def scores(i):
        blk, hp = i // 4, i % 4
        qt = tokens_of(qall, blk, blk, hp) * jnp.asarray(0.125, BF)
        qt_s[blk, hp] = qt
        k = k_ref[pair_of(blk), :, columns(hp)]
        for hh in range(2):
            sbuf[i % 2, hh] = dot(k, only(qt, hh))

    def forward(i):
        blk, hp = i // 4, i % 4
        pair = pair_of(blk)
        now = [sbuf[i % 2, hh] for hh in range(2)]
        scores(jnp.minimum(i + 1, 11))
        for hh in range(2):
            m = jnp.max(now[hh], axis=0, keepdims=True)
            p = jnp.exp(now[hh] - m).astype(BF)
            ep[blk, 2 * hp + hh, :, 256:512] = p
            o = dot(vkt[pair, 2 * hp + hh], p)
            ob[blk, hp, 64 * hh : 64 * hh + 64, :] = o[0:64].astype(BF)
            ob[blk, hp, 128 + 64 * hh : 192 + 64 * hh, :] = o[64:128].astype(BF)
            st[blk, 2 * hp + hh, 0:1, :] = m
            st[blk, 2 * hp + hh, 1:2, :] = o[128:129]

    def backward(i):
        blk, hp = (i // 4 + 1) % 3, i % 4
        pair = pair_of(blk)
        gt = tokens_of(gall, jnp.where(blk == 2, third_slot, blk), blk, hp)
        gt_s[blk, hp] = gt
        v = v_ref[pair, :, columns(hp)]
        dps = [dot(v, only(gt, hh)) for hh in range(2)]
        for hh in range(2):
            o = ob[blk, hp, 64 * hh : 64 * hh + 64, :].astype(F32)
            r = jnp.sum(gt[64 * hh : 64 * hh + 64].astype(F32) * o, axis=0, keepdims=True)
            d = r / st[blk, 2 * hp + hh, 1:2, :]
            e = (ep[blk, 2 * hp + hh, :, 256:512].astype(F32) * (dps[hh] - d)).astype(BF)
            ep[blk, 2 * hp + hh, :, 0:256] = e
            a = dot(vkt[pair, 2 * hp + hh, 64:128, :], e)
            ab[blk, hp, 64 * hh : 64 * hh + 64, :] = a.astype(BF)
            sd[blk, 2 * hp + hh, 0:1, :] = d

    def to_owners(which, wide, narrow, halves=(0, 1)):
        @pl.loop(1, CHIPS)
        def _(i):
            p = peer_of(me, i)
            for half, cols, sems in ((0, wide, big_s), (1, narrow, small_s)):
                if half in halves:

                    @pl.when(p // 16 == half)
                    def _():
                        pltpu.make_async_remote_copy(
                            comb.at[which, p, :, pl.ds(0, cols)], rsbuf.at[which, me, :, pl.ds(0, cols)],
                            sems.at[which], rs_r.at[which], device_id={"seq": p}, device_id_type=MESH,
                        ).start()

        for half in halves:

            @pl.when(me // 16 == half)
            def _():
                rsbuf[which, me] = comb[which, me]

    def owners_landed(which, wide, narrow):
        @pl.when(early)
        def _():
            pending(rsbuf.at[which, pl.ds(0, 31), :, pl.ds(0, wide)], big_s.at[which], rs_r.at[which]).wait_recv()
            pending(comb.at[which, pl.ds(0, 15), :, pl.ds(0, wide)], big_s.at[which], rs_r.at[which]).wait_send()
            pending(comb.at[which, pl.ds(0, 16), :, pl.ds(0, narrow)], small_s.at[which], rs_r.at[which]).wait_send()

        @pl.when(jnp.logical_not(early))
        def _():
            pending(rsbuf.at[which, pl.ds(0, 31), :, pl.ds(0, narrow)], big_s.at[which], rs_r.at[which]).wait_recv()
            pending(comb.at[which, pl.ds(0, 16), :, pl.ds(0, wide)], big_s.at[which], rs_r.at[which]).wait_send()
            pending(comb.at[which, pl.ds(0, 15), :, pl.ds(0, narrow)], small_s.at[which], rs_r.at[which]).wait_send()

    def place_of(i):
        first = jnp.where(i < 4, 0, 2)
        hp = jnp.where(i < 4, i, 2 * core + i - 4)
        return first, hp, pl.ds(jnp.where(i < 4, 0, 16), 16), columns(jnp.where(i < 4, i, i - 4))

    def combine_forward(first, last):
        @pl.loop(first, last)
        def _(i):
            blk, hp, chips, cols = place_of(i)
            os, bs = [], []
            for hh in range(2):
                a, b = st[blk, 2 * hp + hh], stsib[2 * i + hh]
                m = jnp.maximum(a[0:1], b[0:1])
                wa, wb = jnp.exp(a[0:1] - m), jnp.exp(b[0:1] - m)
                cst[2 * i + hh, 0:1, :] = m
                cst[2 * i + hh, 1:2, :] = wa * a[1:2] + wb * b[1:2]
                cst[2 * i + hh, 2:3, :] = wa
                cst[2 * i + hh, 3:4, :] = wb
                for out, lo in ((os, 64 * hh), (bs, 128 + 64 * hh)):
                    x = ob[blk, hp, lo : lo + 64, :].astype(F32)
                    y = obsib[i, lo : lo + 64, :].astype(F32)
                    out.append(wa * x + wb * y)
            oc[i] = jnp.concatenate(os, axis=0).astype(BF)
            comb[0, chips, :, cols] = oc[i].T.reshape(16, 16, 128)
            comb[1, chips, :, cols] = jnp.concatenate(bs, axis=0).T.astype(BF).reshape(16, 16, 128)

        if first == 0:
            m8, l8 = cst[0:8, 0, :], cst[0:8, 1, :]
        else:
            none = jnp.zeros((4, 256), F32)
            m8 = jnp.concatenate([cst[8:12, 0, :], none], axis=0)
            l8 = jnp.concatenate([cst[8:12, 1, :], none], axis=0)
        pad = jnp.zeros((128 - 48, 256), F32)
        tile = jnp.concatenate([*split3(m8), *split3(l8), pad], axis=0).T.astype(BF).reshape(16, 16, 128)
        if first == 0:
            comb[0, 0:16, :, 512:640] = tile
        else:
            comb[0, 16:32, :, 256:384] = tile

    def combine_backward():
        @pl.loop(0, 6)
        def _(i):
            blk, hp, chips, cols = place_of(i)
            parts = []
            for hh in range(2):
                c = cst[2 * i + hh]
                l, wa, wb = c[1:2], c[2:3], c[3:4]
                da, db = sd[blk, 2 * hp + hh, 0:1, :], sdsib[2 * i + hh, 0:1, :]
                lo, bo = 64 * hh, 128 + 64 * hh
                gt = gt_s[blk, hp, lo : lo + 64, :].astype(F32)
                d = jnp.sum(gt * oc[i, lo : lo + 64, :].astype(F32), axis=0, keepdims=True) / l
                xa, xb = ab[blk, hp, lo : lo + 64, :].astype(F32), ob[blk, hp, bo : bo + 64, :].astype(F32)
                ya, yb = absib[i, lo : lo + 64, :].astype(F32), obsib[i, bo : bo + 64, :].astype(F32)
                parts.append(wa * (xa + (da - d) * xb) + wb * (ya + (db - d) * yb))
            comb[2, chips, :, cols] = jnp.concatenate(parts, axis=0).astype(BF).T.reshape(16, 16, 128)

    stat_cols = pl.ds(pl.multiple_of(jnp.where(early, 512, 256), 128), 128)
    width = jnp.where(early, 512, 256)
    inside = lax.broadcasted_iota(jnp.int32, (16, 512), 1) < width

    def expand(first):
        return onehot((128, 512), lambda r, c: (r >= first) & (r < first + 24) & ((r - first) % 8 == c // 64))

    def repeat(first):
        return onehot((128, 128), lambda r, c: (r >= first) & (r < first + 24) & ((r - first) % 8 == c % 8))

    def own_attended():
        s = rsbuf[0, :, :, stat_cols].reshape(512, 128)
        m_all = dot(s, expand(0)).reshape(CHIPS, 16, 512)
        wts[...] = jnp.exp(m_all - jnp.max(m_all, axis=0, keepdims=True))
        l_all = dot(s, expand(24)).reshape(CHIPS, 16, 512)
        l_sum = jnp.sum(wts[...] * l_all, axis=0)
        inv = 1.0 / jnp.where(inside, l_sum, 1.0)
        att = jnp.sum(wts[...] * rsbuf[0, :, :, 0:512].astype(F32), axis=0)
        att = jnp.where(inside, att * inv, 0.0)
        third_g = gall[third_slot, me, :, pl.ds(pl.multiple_of(256 * core, 128), 256)]
        third_g = jnp.concatenate([third_g, jnp.zeros((16, 256), BF)], axis=1)
        g = jnp.where(early, gmine[...].astype(F32), third_g.astype(F32))
        dprod = jnp.where(inside[None], rsbuf[0, :, :, 0:512].astype(F32) * g[None], 0.0).reshape(512, 512)
        high = dprod.astype(BF)
        low = (dprod - high.astype(F32)).astype(BF)
        prods = split3(g * att)
        same = onehot((512, 512), lambda r, c: r // 64 == c // 64)
        to8 = onehot((512, 128), lambda r, c: r // 64 == c % 8)
        delta = sum(dot(x.astype(BF), same) for x in prods)
        d_dev = (dot(high, same) + dot(low, same)).reshape(CHIPS, 16, 512)
        ddev[...] = d_dev / jnp.where(inside[None], l_all, 1.0) - delta[None]
        delta8 = sum(dot(x.astype(BF), to8) for x in prods)
        own[...] = inv
        m8 = dot(s, repeat(0)).reshape(CHIPS, 16, 128)
        l8 = dot(s, repeat(24)).reshape(CHIPS, 16, 128)
        top8 = jnp.max(m8, axis=0)
        l8 = jnp.sum(jnp.exp(m8 - top8[None]) * l8, axis=0)
        inv8 = 1.0 / jnp.where(l8 > 0, l8, 1.0)
        lane = lax.broadcasted_iota(jnp.int32, (16, 128), 1) // 8
        tile = jnp.zeros((16, 128), F32)
        for n, term in enumerate((*split3(top8), *split3(inv8), *split3(delta8))):
            tile = jnp.where(lane == n, term, tile)
        agbuf[0, me] = tile.astype(BF)
        spread(agbuf.at[0, me], agbuf.at[0], ag_s, ag_r)
        xs[0] = att.astype(BF)

    def own_queries():
        a = rsbuf[2, :, :, 0:512].astype(F32)
        b = rsbuf[1, :, :, 0:512].astype(F32)
        t = jnp.sum(wts[...] * (a + ddev[...] * b), axis=0)
        xs[1] = jnp.where(inside, t * own[...] * 0.125, 0.0).astype(BF)

    def settle(which):
        @pl.when(jnp.logical_not(early))
        def _():
            swap = across(xs.at[which, :, pl.ds(0, 256)], xr.at[which], 8 + which)
            swap.start()
            swap.wait()
            mine, their = xs[which, :, 0:256].astype(F32), xr[which].astype(F32)
            both = jnp.concatenate(
                [jnp.where(core == 0, mine, their), jnp.where(core == 0, their, mine)], axis=1
            )
            xs[which] = jnp.where(mine_longer, both, 0.0).astype(BF)

    send_q = across(qall.at[0], qall.at[1], 0)
    send_g = across(gall.at[0], gall.at[1], 1)
    obs_1 = across(ob.at[1], obsib.at[pl.ds(0, 4)], 2)
    st_1 = across(st.at[1], stsib.at[pl.ds(0, 8)], 3)
    obs_2 = across(ob.at[2, pl.ds(2 * other, 2)], obsib.at[pl.ds(4, 2)], 4)
    st_2 = across(st.at[2, pl.ds(4 * other, 4)], stsib.at[pl.ds(8, 4)], 5)
    abs_1 = across(ab.at[1], absib.at[pl.ds(0, 4)], 6)
    sd_1 = across(sd.at[1], sdsib.at[pl.ds(0, 8)], 7)
    abs_2 = across(ab.at[2, pl.ds(2 * other, 2)], absib.at[pl.ds(4, 2)], 10)
    sd_2 = across(sd.at[2, pl.ds(4 * other, 4)], sdsib.at[pl.ds(8, 4)], 11)

    landed(qall.at[0], gat_s.at[0], gat_r.at[0])
    send_q.start()
    scores(0)

    @pl.loop(0, 12)
    def _(i):
        @pl.when(i == 3)
        def _():
            send_q.wait()

            @pl.loop(16, CHIPS)
            def _(chip):
                qall[2, chip] = jnp.where(mine_longer, qall[0, chip], qall[1, chip])

        forward(i)

        @pl.when(i == 7)
        def _():
            obs_1.start()
            st_1.start()

    obs_2.start()
    st_2.start()
    obs_1.wait()
    st_1.wait()
    combine_forward(0, 4)
    to_owners(0, 640, 384, (0,))
    obs_2.wait()
    st_2.wait()
    combine_forward(4, 6)
    to_owners(0, 640, 384, (1,))
    landed(gall.at[0], gat_s.at[1], gat_r.at[1])
    send_g.start()
    send_g.wait()

    @pl.loop(0, 12, unroll=2)
    def _(i):
        backward(i)

        @pl.when(i == 3)
        def _():
            abs_1.start()
            sd_1.start()

        @pl.when(i == 7)
        def _():
            abs_2.start()
            sd_2.start()
            to_owners(1, 512, 256)

        @pl.when(i == 9)
        def _():
            owners_landed(0, 640, 384)
            own_attended()

    abs_1.wait()
    sd_1.wait()
    abs_2.wait()
    sd_2.wait()
    combine_backward()
    to_owners(2, 512, 256)

    settle(0)
    third_valid = token < 512 - pad_ref[core]
    crecv[head] = jnp.where(third_valid, xs[0].astype(F32), 0.0).astype(BF)
    for j in (1, 2, 3):
        to_head(lambda p: crecv.at[head], crecv, csem, j).start()

    landed(agbuf.at[0], ag_s, ag_r)
    send_ag = across(agbuf.at[0], agbuf.at[1], 12)
    send_ag.start()
    send_ag.wait()

    for blk in range(3):
        if blk < 2:
            t = agbuf[blk, 0:16].reshape(256, 128).T.astype(F32)
            terms = [t[8 * n : 8 * n + 8] for n in range(9)]
        else:
            t0 = agbuf[core, 16:32].reshape(256, 128).T.astype(F32)
            t1 = agbuf[other, 16:32].reshape(256, 128).T.astype(F32)
            terms = [
                jnp.concatenate([t0[8 * n : 8 * n + 4], t1[8 * n : 8 * n + 4]], axis=0) for n in range(9)
            ]
        top, inv, delta = (terms[n] + terms[n + 1] + terms[n + 2] for n in (0, 3, 6))
        c = jnp.exp(st[blk, :, 0, :] - top) * inv
        gap = sd[blk, :, 0, :] - delta
        for h in range(8):
            gst[blk, h, 0:1, :] = c[h : h + 1]
            gst[blk, h, 1:2, :] = gap[h : h + 1]

    @pl.loop(0, 4)
    def _(hp):
        zero64 = jnp.zeros((64, 512), BF)
        zero256 = jnp.zeros((64, 256), BF)
        outs = []
        for blk in range(3):
            acc = None
            for hh in range(2):
                c, gap = gst[blk, 2 * hp + hh, 0:1, :], gst[blk, 2 * hp + hh, 1:2, :]
                qh = qt_s[blk, hp, 64 * hh : 64 * hh + 64, :].astype(F32)
                gh = gt_s[blk, hp, 64 * hh : 64 * hh + 64, :].astype(F32)
                qc = c * qh
                wk = jnp.concatenate([qc.astype(BF), (gap * qc).astype(BF)], axis=1)
                wv = jnp.concatenate([zero256, (c * gh).astype(BF)], axis=1)
                rows = [wk, zero64, wv, zero64] if hh == 0 else [zero64, wk, zero64, wv]
                part = dot_nt(ep[blk, 2 * hp + hh], jnp.concatenate(rows, axis=0))
                acc = part if acc is None else acc + part
            outs.append(acc)
        mine = outs[0] + jnp.where(mine_longer, outs[2], 0.0)
        theirs = outs[1] + jnp.where(mine_longer, 0.0, outs[2])
        dk_ref[core, :, columns(hp)] = mine[:, 0:128].astype(BF)
        dv_ref[core, :, columns(hp)] = mine[:, 128:256].astype(BF)
        dk_ref[other, :, columns(hp)] = theirs[:, 0:128].astype(BF)
        dv_ref[other, :, columns(hp)] = theirs[:, 128:256].astype(BF)

    for j in (1, 2, 3):
        from_head(lambda p: crecv.at[head], crecv, csem, j).wait()
    pick = onehot((4, 16), lambda r, c: c == r + 4 * head)
    for p in range(4):
        ctx_ref[:, p * 512 : (p + 1) * 512] = dot(pick, crecv[p]).astype(BF)

    owners_landed(1, 512, 256)
    owners_landed(2, 512, 256)
    own_queries()
    settle(1)
    dq_ref[...] = xs[1]


def local(queries, keys, values, grad_out, pad_counts):
    vmem = pl.BlockSpec(memory_space=pltpu.VMEM)
    dma = pltpu.SemaphoreType.DMA
    return pl.pallas_call(
        kernel,
        out_shape=(
            jax.ShapeDtypeStruct(grad_out.shape, BF),
            jax.ShapeDtypeStruct(queries.shape, BF),
            jax.ShapeDtypeStruct(keys.shape, BF),
            jax.ShapeDtypeStruct(values.shape, BF),
        ),
        in_specs=[pl.BlockSpec(memory_space=pltpu.SMEM)] + [pl.BlockSpec(memory_space=pl.ANY)] * 4,
        out_specs=(vmem,) * 4,
        scratch_shapes=[
            pltpu.VMEM(queries.shape, BF),
            pltpu.VMEM(keys.shape, BF),
            pltpu.VMEM(values.shape, BF),
            pltpu.VMEM(grad_out.shape, BF),
            pltpu.VMEM((4, 16, 512), BF),
            pltpu.VMEM((4, 16, 512), BF),
            pltpu.VMEM((16, 512), BF),
            pltpu.VMEM((3, CHIPS, 16, 512), BF),
            pltpu.VMEM((2, CHIPS, 16, 512), BF),
            pltpu.VMEM((3, 4, 128, 256), BF),
            pltpu.VMEM((3, 4, 128, 256), BF),
            pltpu.VMEM((2, 8, 144, 512), BF),
            pltpu.VMEM((3, 8, 512, 512), BF),
            pltpu.VMEM((3, 4, 256, 256), BF),
            pltpu.VMEM((3, 4, 128, 256), BF),
            pltpu.VMEM((3, 8, 8, 256), F32),
            pltpu.VMEM((3, 8, 8, 256), F32),
            pltpu.VMEM((6, 256, 256), BF),
            pltpu.VMEM((6, 128, 256), BF),
            pltpu.VMEM((12, 8, 256), F32),
            pltpu.VMEM((12, 8, 256), F32),
            pltpu.VMEM((12, 8, 256), F32),
            pltpu.VMEM((6, 128, 256), BF),
            pltpu.VMEM((2, 2, 512, 256), F32),
            pltpu.VMEM((3, CHIPS, 16, 640), BF),
            pltpu.VMEM((3, CHIPS, 16, 640), BF),
            pltpu.VMEM((CHIPS, 16, 512), F32),
            pltpu.VMEM((16, 512), F32),
            pltpu.VMEM((CHIPS, 16, 512), F32),
            pltpu.VMEM((2, CHIPS, 16, 128), BF),
            pltpu.VMEM((3, 8, 8, 256), F32),
            pltpu.VMEM((2, 16, 512), BF),
            pltpu.VMEM((2, 16, 256), BF),
            pltpu.VMEM((4, 16, 512), BF),
            dma((4,)),
            dma((8,)),
            dma((2,)),
            dma((2,)),
            dma((13,)),
            dma((13,)),
            dma((3,)),
            dma((3,)),
            dma((3,)),
            dma(()),
            dma(()),
            dma((8,)),
        ],
        compiler_params=pltpu.CompilerParams(
            collective_id=0, has_side_effects=True, vmem_limit_bytes=50 * 2**20
        ),
    )(pad_counts, queries, keys, values, grad_out)


def solution(mesh):
    return jax.shard_map(
        local,
        mesh=mesh,
        in_specs=(
            P(("grp", "seq"), "head"),
            P(None, ("grp", "seq"), "head"),
            P(None, ("grp", "seq"), "head"),
            P(("grp", "seq", "head"), None),
            P(),
        ),
        out_specs=(
            P(("grp", "seq", "head"), None),
            P(("grp", "seq"), "head"),
            P(None, ("grp", "seq"), "head"),
            P(None, ("grp", "seq"), "head"),
        ),
        check_vma=False,
    )
```

```python
import jax
import jax.numpy as jnp
from jax import lax
from jax.experimental import pallas as pl
from jax.experimental.pallas import tpu as pltpu
from jax.sharding import PartitionSpec as P

MESH = pl.DeviceIdType.MESH
CHIPS = 32
PEERS = CHIPS - 1
BF = jnp.bfloat16
F32 = jnp.float32


def peer_of(me, i):
    i = 32 - i
    x, z, y = me // 8, (me // 4) % 2, me % 4
    return ((x + i // 8) % 4) * 8 + ((z + (i // 4) % 2) % 2) * 4 + (y + i % 4) % 4


def dot(a, b):
    return lax.dot_general(a, b, (((1,), (0,)), ((), ())), preferred_element_type=F32)


def dot_nt(a, b):
    return lax.dot_general(a, b, (((1,), (1,)), ((), ())), preferred_element_type=F32)


def columns(hp):
    return pl.ds(pl.multiple_of(hp * 128, 128), 128)


def split3(x):
    a = x.astype(BF).astype(F32)
    b = (x - a).astype(BF).astype(F32)
    return a, b, (x - a - b).astype(BF).astype(F32)


def onehot(shape, rule):
    r = lax.broadcasted_iota(jnp.int32, shape, 0)
    c = lax.broadcasted_iota(jnp.int32, shape, 1)
    return rule(r, c).astype(BF)


def kernel(
    pad_ref, q_hbm, k_hbm, v_hbm, g_hbm,
    ctx_ref, dq_ref, dk_ref, dv_ref,
    q_ref, k_ref, v_ref, g_ref,
    gsend, grecv, gmine, qall, gall, qt_s, gt_s, vkt, ep, ob, ab,
    st, sd, obsib, absib, stsib, sdsib, cst, oc, sbuf, comb, rsbuf, wts, own, ddev, agbuf, gst, xs, xr, crecv,
    lsem, hsem, gat_s, gat_r, sib_s, sib_r, big_s, small_s, rs_r, ag_s, ag_r, csem,
):
    core = lax.axis_index("grp")
    me = lax.axis_index("seq")
    head = lax.axis_index("head")
    other = 1 - core
    sibling = {"grp": other}
    early = me < 16

    barrier = pltpu.get_barrier_semaphore()

    @pl.loop(1, CHIPS)
    def _(i):
        pl.semaphore_signal(barrier, inc=1, device_id={"seq": peer_of(me, i)}, device_id_type=MESH)

    pl.semaphore_signal(barrier, inc=1, device_id=sibling, device_id_type=MESH)
    for j in (1, 2, 3):
        pl.semaphore_signal(barrier, inc=1, device_id={"head": (head + j) % 4}, device_id_type=MESH)

    loads = [
        pltpu.make_async_copy(src, dst, lsem.at[n])
        for n, (src, dst) in enumerate(((g_hbm, g_ref), (q_hbm, q_ref), (k_hbm, k_ref), (v_hbm, v_ref)))
    ]
    for load in loads:
        load.start()
    for load in loads:
        load.wait()

    @pl.loop(0, 8)
    def _(i):
        pair, hp = i // 4, i % 4
        kt = k_ref[pair, :, columns(hp)].T
        vt = v_ref[pair, :, columns(hp)].T
        for hh in range(2):
            vkt[pair, 2 * hp + hh, 0:64, :] = vt[64 * hh : 64 * hh + 64]
            vkt[pair, 2 * hp + hh, 64:128, :] = kt[64 * hh : 64 * hh + 64]
            vkt[pair, 2 * hp + hh, 128:144, :] = jnp.ones((16, 512), BF)

    place = onehot((16, 4), lambda r, c: r == c + 4 * head)
    for p in range(4):
        gsend[p] = dot(place, g_ref[:, p * 512 : (p + 1) * 512]).astype(BF)

    pl.semaphore_wait(barrier, PEERS + 4)

    def to_head(src, dst, sems, j):
        p = (head + j) % 4
        return pltpu.make_async_remote_copy(
            src(p), dst.at[head], sems.at[j], sems.at[4 + head], device_id={"head": p}, device_id_type=MESH
        )

    def from_head(src, dst, sems, j):
        p = (head + j) % 4
        return pltpu.make_async_remote_copy(
            src(p), dst.at[p], sems.at[j], sems.at[4 + p], device_id={"head": p}, device_id_type=MESH
        )

    def pending(ref, send, recv):
        return pltpu.make_async_remote_copy(ref, ref, send, recv, device_id=sibling, device_id_type=MESH)

    def spread(src, dst, send, recv):
        @pl.loop(1, CHIPS)
        def _(i):
            pltpu.make_async_remote_copy(
                src, dst.at[me], send, recv, device_id={"seq": peer_of(me, i)}, device_id_type=MESH
            ).start()

    def landed(dst, send, recv):
        copy = pending(dst.at[pl.ds(0, PEERS)], send, recv)
        copy.wait_recv()
        copy.wait_send()

    def across(src, dst, k):
        return pltpu.make_async_remote_copy(
            src, dst, sib_s.at[k], sib_r.at[k], device_id=sibling, device_id_type=MESH
        )

    for j in (1, 2, 3):
        to_head(lambda p: gsend.at[p], grecv, hsem, j).start()
    spread(q_ref, qall.at[0], gat_s.at[0], gat_r.at[0])
    qall[0, me] = q_ref[...]
    grecv[head] = gsend[head]
    for j in (1, 2, 3):
        from_head(lambda p: gsend.at[p], grecv, hsem, j).wait()

    token = lax.broadcasted_iota(jnp.int32, (16, 512), 0) + me * 16
    gsum = (grecv[0].astype(F32) + grecv[1].astype(F32)) + (grecv[2].astype(F32) + grecv[3].astype(F32))
    gown = jnp.where(token < 512 - pad_ref[core], gsum, 0.0).astype(BF)
    gmine[...] = gown
    spread(gmine, gall.at[0], gat_s.at[1], gat_r.at[1])
    gall[0, me] = gown

    longer = jnp.where(pad_ref[1] < pad_ref[0], 1, 0)
    mine_longer = longer == core
    third_slot = jnp.where(mine_longer, 0, 1)

    row = lax.broadcasted_iota(jnp.int32, (128, 256), 0)

    def only(t, hh):
        return jnp.where((row < 64) if hh == 0 else (row >= 64), t, jnp.zeros((), t.dtype))

    def pair_of(blk):
        return jnp.where(blk == 0, core, jnp.where(blk == 1, other, longer))

    def tokens_of(buf, slot, blk, hp):
        return buf[slot, pl.ds(16 * (blk // 2), 16), :, columns(hp)].reshape(256, 128).T

    def scores(i):
        blk, hp = i // 4, i % 4
        qt = tokens_of(qall, blk, blk, hp) * jnp.asarray(0.125, BF)
        qt_s[blk, hp] = qt
        k = k_ref[pair_of(blk), :, columns(hp)]
        for hh in range(2):
            sbuf[i % 2, hh] = dot(k, only(qt, hh))

    def forward(i):
        blk, hp = i // 4, i % 4
        pair = pair_of(blk)
        now = [sbuf[i % 2, hh] for hh in range(2)]
        scores(jnp.minimum(i + 1, 11))
        for hh in range(2):
            m = jnp.max(now[hh], axis=0, keepdims=True)
            p = jnp.exp(now[hh] - m).astype(BF)
            ep[blk, 2 * hp + hh, :, 256:512] = p
            o = dot(vkt[pair, 2 * hp + hh], p)
            ob[blk, hp, 64 * hh : 64 * hh + 64, :] = o[0:64].astype(BF)
            ob[blk, hp, 128 + 64 * hh : 192 + 64 * hh, :] = o[64:128].astype(BF)
            st[blk, 2 * hp + hh, 0:1, :] = m
            st[blk, 2 * hp + hh, 1:2, :] = o[128:129]

    def backward(i):
        blk, hp = (i // 4 + 1) % 3, i % 4
        pair = pair_of(blk)
        gt = tokens_of(gall, jnp.where(blk == 2, third_slot, blk), blk, hp)
        gt_s[blk, hp] = gt
        v = v_ref[pair, :, columns(hp)]
        dps = [dot(v, only(gt, hh)) for hh in range(2)]
        for hh in range(2):
            o = ob[blk, hp, 64 * hh : 64 * hh + 64, :].astype(F32)
            r = jnp.sum(gt[64 * hh : 64 * hh + 64].astype(F32) * o, axis=0, keepdims=True)
            d = r / st[blk, 2 * hp + hh, 1:2, :]
            e = (ep[blk, 2 * hp + hh, :, 256:512].astype(F32) * (dps[hh] - d)).astype(BF)
            ep[blk, 2 * hp + hh, :, 0:256] = e
            a = dot(vkt[pair, 2 * hp + hh, 64:128, :], e)
            ab[blk, hp, 64 * hh : 64 * hh + 64, :] = a.astype(BF)
            sd[blk, 2 * hp + hh, 0:1, :] = d

    def to_owners(which, wide, narrow, halves=(0, 1)):
        @pl.loop(1, CHIPS)
        def _(i):
            p = peer_of(me, i)
            for half, cols, sems in ((0, wide, big_s), (1, narrow, small_s)):
                if half in halves:

                    @pl.when(p // 16 == half)
                    def _():
                        pltpu.make_async_remote_copy(
                            comb.at[which, p, :, pl.ds(0, cols)], rsbuf.at[which, me, :, pl.ds(0, cols)],
                            sems.at[which], rs_r.at[which], device_id={"seq": p}, device_id_type=MESH,
                        ).start()

        for half in halves:

            @pl.when(me // 16 == half)
            def _():
                rsbuf[which, me] = comb[which, me]

    def owners_landed(which, wide, narrow):
        @pl.when(early)
        def _():
            pending(rsbuf.at[which, pl.ds(0, 31), :, pl.ds(0, wide)], big_s.at[which], rs_r.at[which]).wait_recv()
            pending(comb.at[which, pl.ds(0, 15), :, pl.ds(0, wide)], big_s.at[which], rs_r.at[which]).wait_send()
            pending(comb.at[which, pl.ds(0, 16), :, pl.ds(0, narrow)], small_s.at[which], rs_r.at[which]).wait_send()

        @pl.when(jnp.logical_not(early))
        def _():
            pending(rsbuf.at[which, pl.ds(0, 31), :, pl.ds(0, narrow)], big_s.at[which], rs_r.at[which]).wait_recv()
            pending(comb.at[which, pl.ds(0, 16), :, pl.ds(0, wide)], big_s.at[which], rs_r.at[which]).wait_send()
            pending(comb.at[which, pl.ds(0, 15), :, pl.ds(0, narrow)], small_s.at[which], rs_r.at[which]).wait_send()

    def place_of(i):
        first = jnp.where(i < 4, 0, 2)
        hp = jnp.where(i < 4, i, 2 * core + i - 4)
        return first, hp, pl.ds(jnp.where(i < 4, 0, 16), 16), columns(jnp.where(i < 4, i, i - 4))

    def combine_forward(first, last):
        @pl.loop(first, last)
        def _(i):
            blk, hp, chips, cols = place_of(i)
            os, bs = [], []
            for hh in range(2):
                a, b = st[blk, 2 * hp + hh], stsib[2 * i + hh]
                m = jnp.maximum(a[0:1], b[0:1])
                wa, wb = jnp.exp(a[0:1] - m), jnp.exp(b[0:1] - m)
                cst[2 * i + hh, 0:1, :] = m
                cst[2 * i + hh, 1:2, :] = wa * a[1:2] + wb * b[1:2]
                cst[2 * i + hh, 2:3, :] = wa
                cst[2 * i + hh, 3:4, :] = wb
                for out, lo in ((os, 64 * hh), (bs, 128 + 64 * hh)):
                    x = ob[blk, hp, lo : lo + 64, :].astype(F32)
                    y = obsib[i, lo : lo + 64, :].astype(F32)
                    out.append(wa * x + wb * y)
            oc[i] = jnp.concatenate(os, axis=0).astype(BF)
            comb[0, chips, :, cols] = oc[i].T.reshape(16, 16, 128)
            comb[1, chips, :, cols] = jnp.concatenate(bs, axis=0).T.astype(BF).reshape(16, 16, 128)

        if first == 0:
            m8, l8 = cst[0:8, 0, :], cst[0:8, 1, :]
        else:
            none = jnp.zeros((4, 256), F32)
            m8 = jnp.concatenate([cst[8:12, 0, :], none], axis=0)
            l8 = jnp.concatenate([cst[8:12, 1, :], none], axis=0)
        pad = jnp.zeros((128 - 48, 256), F32)
        tile = jnp.concatenate([*split3(m8), *split3(l8), pad], axis=0).T.astype(BF).reshape(16, 16, 128)
        if first == 0:
            comb[0, 0:16, :, 512:640] = tile
        else:
            comb[0, 16:32, :, 256:384] = tile

    def combine_backward():
        @pl.loop(0, 6)
        def _(i):
            blk, hp, chips, cols = place_of(i)
            parts = []
            for hh in range(2):
                c = cst[2 * i + hh]
                l, wa, wb = c[1:2], c[2:3], c[3:4]
                da, db = sd[blk, 2 * hp + hh, 0:1, :], sdsib[2 * i + hh, 0:1, :]
                lo, bo = 64 * hh, 128 + 64 * hh
                gt = gt_s[blk, hp, lo : lo + 64, :].astype(F32)
                d = jnp.sum(gt * oc[i, lo : lo + 64, :].astype(F32), axis=0, keepdims=True) / l
                xa, xb = ab[blk, hp, lo : lo + 64, :].astype(F32), ob[blk, hp, bo : bo + 64, :].astype(F32)
                ya, yb = absib[i, lo : lo + 64, :].astype(F32), obsib[i, bo : bo + 64, :].astype(F32)
                parts.append(wa * (xa + (da - d) * xb) + wb * (ya + (db - d) * yb))
            comb[2, chips, :, cols] = jnp.concatenate(parts, axis=0).astype(BF).T.reshape(16, 16, 128)

    stat_cols = pl.ds(pl.multiple_of(jnp.where(early, 512, 256), 128), 128)
    width = jnp.where(early, 512, 256)
    inside = lax.broadcasted_iota(jnp.int32, (16, 512), 1) < width

    def expand(first):
        return onehot((128, 512), lambda r, c: (r >= first) & (r < first + 24) & ((r - first) % 8 == c // 64))

    def repeat(first):
        return onehot((128, 128), lambda r, c: (r >= first) & (r < first + 24) & ((r - first) % 8 == c % 8))

    def own_attended():
        s = rsbuf[0, :, :, stat_cols].reshape(512, 128)
        m_all = dot(s, expand(0)).reshape(CHIPS, 16, 512)
        wts[...] = jnp.exp(m_all - jnp.max(m_all, axis=0, keepdims=True))
        l_all = dot(s, expand(24)).reshape(CHIPS, 16, 512)
        l_sum = jnp.sum(wts[...] * l_all, axis=0)
        inv = 1.0 / jnp.where(inside, l_sum, 1.0)
        att = jnp.sum(wts[...] * rsbuf[0, :, :, 0:512].astype(F32), axis=0)
        att = jnp.where(inside, att * inv, 0.0)
        third_g = gall[third_slot, me, :, pl.ds(pl.multiple_of(256 * core, 128), 256)]
        third_g = jnp.concatenate([third_g, jnp.zeros((16, 256), BF)], axis=1)
        g = jnp.where(early, gmine[...].astype(F32), third_g.astype(F32))
        dprod = jnp.where(inside[None], rsbuf[0, :, :, 0:512].astype(F32) * g[None], 0.0).reshape(512, 512)
        high = dprod.astype(BF)
        low = (dprod - high.astype(F32)).astype(BF)
        prods = split3(g * att)
        same = onehot((512, 512), lambda r, c: r // 64 == c // 64)
        to8 = onehot((512, 128), lambda r, c: r // 64 == c % 8)
        delta = sum(dot(x.astype(BF), same) for x in prods)
        d_dev = (dot(high, same) + dot(low, same)).reshape(CHIPS, 16, 512)
        ddev[...] = d_dev / jnp.where(inside[None], l_all, 1.0) - delta[None]
        delta8 = sum(dot(x.astype(BF), to8) for x in prods)
        own[...] = inv
        m8 = dot(s, repeat(0)).reshape(CHIPS, 16, 128)
        l8 = dot(s, repeat(24)).reshape(CHIPS, 16, 128)
        top8 = jnp.max(m8, axis=0)
        l8 = jnp.sum(jnp.exp(m8 - top8[None]) * l8, axis=0)
        inv8 = 1.0 / jnp.where(l8 > 0, l8, 1.0)
        lane = lax.broadcasted_iota(jnp.int32, (16, 128), 1) // 8
        tile = jnp.zeros((16, 128), F32)
        for n, term in enumerate((*split3(top8), *split3(inv8), *split3(delta8))):
            tile = jnp.where(lane == n, term, tile)
        agbuf[0, me] = tile.astype(BF)
        spread(agbuf.at[0, me], agbuf.at[0], ag_s, ag_r)
        xs[0] = att.astype(BF)

    def own_queries():
        a = rsbuf[2, :, :, 0:512].astype(F32)
        b = rsbuf[1, :, :, 0:512].astype(F32)
        t = jnp.sum(wts[...] * (a + ddev[...] * b), axis=0)
        xs[1] = jnp.where(inside, t * own[...] * 0.125, 0.0).astype(BF)

    def settle(which, between=lambda: None):
        @pl.when(jnp.logical_not(early))
        def _():
            swap = across(xs.at[which, :, pl.ds(0, 256)], xr.at[which], 8 + which)
            swap.start()
            between()
            swap.wait()
            mine, their = xs[which, :, 0:256].astype(F32), xr[which].astype(F32)
            both = jnp.concatenate(
                [jnp.where(core == 0, mine, their), jnp.where(core == 0, their, mine)], axis=1
            )
            xs[which] = jnp.where(mine_longer, both, 0.0).astype(BF)

    send_q = across(qall.at[0], qall.at[1], 0)
    send_g = across(gall.at[0], gall.at[1], 1)
    obs_1 = across(ob.at[1], obsib.at[pl.ds(0, 4)], 2)
    st_1 = across(st.at[1], stsib.at[pl.ds(0, 8)], 3)
    obs_2 = across(ob.at[2, pl.ds(2 * other, 2)], obsib.at[pl.ds(4, 2)], 4)
    st_2 = across(st.at[2, pl.ds(4 * other, 4)], stsib.at[pl.ds(8, 4)], 5)
    abs_1 = across(ab.at[1], absib.at[pl.ds(0, 4)], 6)
    sd_1 = across(sd.at[1], sdsib.at[pl.ds(0, 8)], 7)
    abs_2 = across(ab.at[2, pl.ds(2 * other, 2)], absib.at[pl.ds(4, 2)], 10)
    sd_2 = across(sd.at[2, pl.ds(4 * other, 4)], sdsib.at[pl.ds(8, 4)], 11)

    landed(qall.at[0], gat_s.at[0], gat_r.at[0])
    send_q.start()
    scores(0)

    @pl.loop(0, 12)
    def _(i):
        @pl.when(i == 3)
        def _():
            send_q.wait()

            @pl.loop(16, CHIPS)
            def _(chip):
                qall[2, chip] = jnp.where(mine_longer, qall[0, chip], qall[1, chip])

        forward(i)

        @pl.when(i == 7)
        def _():
            obs_1.start()
            st_1.start()

    obs_2.start()
    st_2.start()
    obs_1.wait()
    st_1.wait()
    combine_forward(0, 4)
    to_owners(0, 640, 384, (0,))
    obs_2.wait()
    st_2.wait()
    combine_forward(4, 6)
    to_owners(0, 640, 384, (1,))
    landed(gall.at[0], gat_s.at[1], gat_r.at[1])
    send_g.start()
    send_g.wait()

    @pl.loop(0, 12, unroll=2)
    def _(i):
        backward(i)

        @pl.when(i == 3)
        def _():
            abs_1.start()
            sd_1.start()

        @pl.when(i == 7)
        def _():
            abs_2.start()
            sd_2.start()
            to_owners(1, 512, 256)

        @pl.when(i == 9)
        def _():
            owners_landed(0, 640, 384)
            own_attended()

    abs_1.wait()
    sd_1.wait()
    abs_2.wait()
    sd_2.wait()
    combine_backward()
    to_owners(2, 512, 256)

    settle(0)
    third_valid = token < 512 - pad_ref[core]
    crecv[head] = jnp.where(third_valid, xs[0].astype(F32), 0.0).astype(BF)
    for j in (1, 2, 3):
        to_head(lambda p: crecv.at[head], crecv, csem, j).start()

    landed(agbuf.at[0], ag_s, ag_r)
    send_ag = across(agbuf.at[0], agbuf.at[1], 12)
    send_ag.start()
    send_ag.wait()

    for blk in range(3):
        if blk < 2:
            t = agbuf[blk, 0:16].reshape(256, 128).T.astype(F32)
            terms = [t[8 * n : 8 * n + 8] for n in range(9)]
        else:
            t0 = agbuf[core, 16:32].reshape(256, 128).T.astype(F32)
            t1 = agbuf[other, 16:32].reshape(256, 128).T.astype(F32)
            terms = [
                jnp.concatenate([t0[8 * n : 8 * n + 4], t1[8 * n : 8 * n + 4]], axis=0) for n in range(9)
            ]
        top, inv, delta = (terms[n] + terms[n + 1] + terms[n + 2] for n in (0, 3, 6))
        c = jnp.exp(st[blk, :, 0, :] - top) * inv
        gap = sd[blk, :, 0, :] - delta
        for h in range(8):
            gst[blk, h, 0:1, :] = c[h : h + 1]
            gst[blk, h, 1:2, :] = gap[h : h + 1]

    @pl.loop(0, 4)
    def _(hp):
        zero64 = jnp.zeros((64, 512), BF)
        zero256 = jnp.zeros((64, 256), BF)
        outs = []
        for blk in range(3):
            acc = None
            for hh in range(2):
                c, gap = gst[blk, 2 * hp + hh, 0:1, :], gst[blk, 2 * hp + hh, 1:2, :]
                qh = qt_s[blk, hp, 64 * hh : 64 * hh + 64, :].astype(F32)
                gh = gt_s[blk, hp, 64 * hh : 64 * hh + 64, :].astype(F32)
                qc = c * qh
                wk = jnp.concatenate([qc.astype(BF), (gap * qc).astype(BF)], axis=1)
                wv = jnp.concatenate([zero256, (c * gh).astype(BF)], axis=1)
                rows = [wk, zero64, wv, zero64] if hh == 0 else [zero64, wk, zero64, wv]
                part = dot_nt(ep[blk, 2 * hp + hh], jnp.concatenate(rows, axis=0))
                acc = part if acc is None else acc + part
            outs.append(acc)
        mine = outs[0] + jnp.where(mine_longer, outs[2], 0.0)
        theirs = outs[1] + jnp.where(mine_longer, 0.0, outs[2])
        dk_ref[core, :, columns(hp)] = mine[:, 0:128].astype(BF)
        dv_ref[core, :, columns(hp)] = mine[:, 128:256].astype(BF)
        dk_ref[other, :, columns(hp)] = theirs[:, 0:128].astype(BF)
        dv_ref[other, :, columns(hp)] = theirs[:, 128:256].astype(BF)

    def context():
        for j in (1, 2, 3):
            from_head(lambda p: crecv.at[head], crecv, csem, j).wait()
        pick = onehot((4, 16), lambda r, c: c == r + 4 * head)
        for p in range(4):
            ctx_ref[:, p * 512 : (p + 1) * 512] = dot(pick, crecv[p]).astype(BF)

    pl.when(early)(context)
    owners_landed(1, 512, 256)
    owners_landed(2, 512, 256)
    own_queries()
    settle(1, context)
    dq_ref[...] = xs[1]


def local(queries, keys, values, grad_out, pad_counts):
    vmem = pl.BlockSpec(memory_space=pltpu.VMEM)
    dma = pltpu.SemaphoreType.DMA
    return pl.pallas_call(
        kernel,
        out_shape=(
            jax.ShapeDtypeStruct(grad_out.shape, BF),
            jax.ShapeDtypeStruct(queries.shape, BF),
            jax.ShapeDtypeStruct(keys.shape, BF),
            jax.ShapeDtypeStruct(values.shape, BF),
        ),
        in_specs=[pl.BlockSpec(memory_space=pltpu.SMEM)] + [pl.BlockSpec(memory_space=pl.ANY)] * 4,
        out_specs=(vmem,) * 4,
        scratch_shapes=[
            pltpu.VMEM(queries.shape, BF),
            pltpu.VMEM(keys.shape, BF),
            pltpu.VMEM(values.shape, BF),
            pltpu.VMEM(grad_out.shape, BF),
            pltpu.VMEM((4, 16, 512), BF),
            pltpu.VMEM((4, 16, 512), BF),
            pltpu.VMEM((16, 512), BF),
            pltpu.VMEM((3, CHIPS, 16, 512), BF),
            pltpu.VMEM((2, CHIPS, 16, 512), BF),
            pltpu.VMEM((3, 4, 128, 256), BF),
            pltpu.VMEM((3, 4, 128, 256), BF),
            pltpu.VMEM((2, 8, 144, 512), BF),
            pltpu.VMEM((3, 8, 512, 512), BF),
            pltpu.VMEM((3, 4, 256, 256), BF),
            pltpu.VMEM((3, 4, 128, 256), BF),
            pltpu.VMEM((3, 8, 8, 256), F32),
            pltpu.VMEM((3, 8, 8, 256), F32),
            pltpu.VMEM((6, 256, 256), BF),
            pltpu.VMEM((6, 128, 256), BF),
            pltpu.VMEM((12, 8, 256), F32),
            pltpu.VMEM((12, 8, 256), F32),
            pltpu.VMEM((12, 8, 256), F32),
            pltpu.VMEM((6, 128, 256), BF),
            pltpu.VMEM((2, 2, 512, 256), F32),
            pltpu.VMEM((3, CHIPS, 16, 640), BF),
            pltpu.VMEM((3, CHIPS, 16, 640), BF),
            pltpu.VMEM((CHIPS, 16, 512), F32),
            pltpu.VMEM((16, 512), F32),
            pltpu.VMEM((CHIPS, 16, 512), F32),
            pltpu.VMEM((2, CHIPS, 16, 128), BF),
            pltpu.VMEM((3, 8, 8, 256), F32),
            pltpu.VMEM((2, 16, 512), BF),
            pltpu.VMEM((2, 16, 256), BF),
            pltpu.VMEM((4, 16, 512), BF),
            dma((4,)),
            dma((8,)),
            dma((2,)),
            dma((2,)),
            dma((13,)),
            dma((13,)),
            dma((3,)),
            dma((3,)),
            dma((3,)),
            dma(()),
            dma(()),
            dma((8,)),
        ],
        compiler_params=pltpu.CompilerParams(
            collective_id=0, has_side_effects=True, vmem_limit_bytes=50 * 2**20
        ),
    )(pad_counts, queries, keys, values, grad_out)


def solution(mesh):
    return jax.shard_map(
        local,
        mesh=mesh,
        in_specs=(
            P(("grp", "seq"), "head"),
            P(None, ("grp", "seq"), "head"),
            P(None, ("grp", "seq"), "head"),
            P(("grp", "seq", "head"), None),
            P(),
        ),
        out_specs=(
            P(("grp", "seq", "head"), None),
            P(("grp", "seq"), "head"),
            P(None, ("grp", "seq"), "head"),
            P(None, ("grp", "seq"), "head"),
        ),
        check_vma=False,
    )
```
